32 devices in a mesh: exp: 8 (over z, y), grp: 4 (over x, core).
Axes of the slice: x: 2, y: 2, z: 4, core: 2. Of those that a mesh axis runs over, the one named last changes fastest.
Arguments:
- tiles: bfloat16 [128, 256, 256], P(('exp', 'grp')), may hold values from -6 to 6
- tile_exposure: int32 [128], P(('exp', 'grp')), may hold values from 0 to 63, as said below
- tile_patch: int32 [128, 4], P(('exp', 'grp')), may hold values from 0 to 7, all different within a row; in each aligned block of 4 rows (0 to 3, 4 to 7, ...) at most 2 rows name the same one
- tile_offset: int32 [128, 4, 2], P(('exp', 'grp')), may hold values from 0 to 256
- coeffs: bfloat16 [64, 10], P(('exp', 'grp')), may hold values from -2 to 2
- inv_var: bfloat16 [64], P(('exp', 'grp')), may hold values from 0.25 to 4
- vert_taps: bfloat16 [10, 41], replicated, may hold values from -1 to 1
- horiz_taps: bfloat16 [10, 41], replicated, may hold values from -1 to 1
Outputs:
- coadd: float32 [8, 512, 512], P('exp', 'grp')
The draws below stay inside these ranges and needn't reach their ends.
Inputs may be any that keep to these rules, and one draw needn't show every extreme that they name: `tile_exposure`: each exposure is named by exactly 128 / 64 tiles. `tile_patch`: the entries of a row differ; among the rows of one device no patch is named by more than 2 rows. `tile_offset`: each tile lies wholly inside each patch listed for it.
All inputs are finite; a program needn't handle non-finite values.
Results may differ from the reference program's by a relative error of at most 0.0041.
Values may be sent and summed in bfloat16 or wider, within the bound.
A program may use at most 128 MiB of HBM per device.

```python
import math
import jax
import jax.numpy as jnp
import numpy as np
from jax import lax

TS = 256
PS = 512
KW = 41
NB = 10
OVL = 4
TILE_DEV = 4
TILES = 128
EXPOSURES = 64
PATCHES = 8
CAP = 2


def draw_tile_exposure(key, part):
    return (jax.random.permutation(key, TILES) % EXPOSURES).astype(jnp.int32)


def place_ends(result, rng, smallest, top_value):
    longest = result.shape.index(max(result.shape))
    spots = []
    for shift in (0, 1):
        where = [jax.random.randint(jax.random.fold_in(rng, axis), (), 0, length) for axis, length in enumerate(result.shape)]
        where[longest] = (where[longest] + shift) % result.shape[longest]
        spots.append(tuple(where))
    return result.at[spots[0]].set(smallest).at[spots[1]].set(top_value)


def level_of(own_key, dims, shards, least, top_value):
    def one(position, parts):
        draws = jax.random.uniform(jax.random.fold_in(jax.random.fold_in(own_key, 6), position), (parts,), jnp.float32, least / len(shards), top_value / len(shards))
        return jnp.repeat(jnp.exp(draws), dims[position] // parts).reshape((-1,) + (1,) * (len(dims) - position - 1))

    level = one(*shards[0])
    for cut in shards[1:]:
        level = level * one(*cut)
    return level


def deal_out(own_key, own, number, rows, number_of, top, limit, slope):
    ranking = jax.random.permutation(own_key, number_of)
    packed, common = portions_of(number_of, rows * top, limit, slope, True), portions_of(number_of, rows * top, limit, slope, False)
    places = jnp.arange(number_of)

    def named(sizes, offset_by):
        used = int((sizes > 0).sum())
        fixed = max(1, used // 4)
        moved = fixed + (places - fixed + offset_by * (used - fixed)) % max(1, number_of - fixed)
        return jnp.zeros((number_of,), jnp.int32).at[ranking[jnp.where(places < fixed, places, moved)]].set(jnp.asarray(sizes, jnp.int32))

    sizes = jnp.where(number % 4 == 0, named(packed, number // 4), named(common, number - number // 4 - 1))
    mixed = jax.random.permutation(jax.random.fold_in(own, 3), number_of)
    donor, sink = mixed[0:number_of // 2 * 2:2], mixed[1:number_of // 2 * 2:2]
    room = jnp.minimum(sizes[donor] - 1, limit - sizes[sink]) // 2
    room = jnp.where((donor == ranking[0]) | (sink == ranking[0]) | (sizes[sink] == 0), 0, jnp.maximum(room, 0))
    moved = jax.random.randint(jax.random.fold_in(own, 4), (number_of // 2,), 0, 1 << 20) % (room + 1)
    sizes = sizes.at[donor].add(-moved).at[sink].add(moved)
    members = jnp.searchsorted(jnp.cumsum(sizes), jnp.arange(rows * top), side="right").astype(jnp.int32)
    table = members.reshape(top, rows).T
    table = table[jax.random.permutation(jax.random.fold_in(own, 1), rows)]
    offset_by = jax.random.randint(jax.random.fold_in(own, 2), (rows, 1), 0, top)
    return jnp.take_along_axis(table, (jnp.arange(top)[None, :] + offset_by) % top, axis=1)


def portions_of(count, total, reach, skew, full):
    weights = [(1 << 20) // math.isqrt(standing ** skew) + 1 for standing in range(1, count + 1)]
    largest = reach if full else min(reach, max(-(-total // count), total * weights[0] // sum(weights)))
    least = 1 if total - largest >= count - 1 else 0
    given, surplus = [largest] + [least] * (count - 1), total - largest - least * (count - 1)
    while surplus > 0:
        movable = [i for i in range(1, count) if given[i] < largest] or [i for i in range(1, count) if given[i] < reach]
        pool, remaining = sum([weights[i] for i in movable]), surplus
        for i in movable:
            more = min(reach - given[i], max(1, remaining * weights[i] // pool), surplus)
            given[i] = given[i] + more
            surplus = surplus - more
    return np.array(given)


def scatter_about(key, extent, width, reach, split=(), held_as=jnp.bfloat16):
    factor_of = level_of(key, extent, split, -0.22, 0.18) if split else 1.0
    entries = jax.random.normal(key, extent, jnp.float32) * width * factor_of
    return jnp.minimum(jnp.maximum(entries, -reach), reach).astype(held_as)


def setup_inputs(seed: int = 0) -> dict:
    key_list = jax.random.split(jax.random.key(seed), 9)
    tiles = scatter_about(key_list[0], (TILES, TS, TS), 1.0, 6.0, ((0, 32),))
    tile_exposure = draw_tile_exposure(jax.random.fold_in(key_list[8], 71), 0)
    tile_patch_keys = jax.random.split(jax.random.fold_in(key_list[2], 1), TILES // TILE_DEV)
    tile_patch_turns = jax.random.permutation(jax.random.fold_in(key_list[2], 3), TILES // TILE_DEV)
    tile_patch = jax.vmap(lambda own, number: deal_out(jax.random.fold_in(key_list[2], 2), own, number, TILE_DEV, PATCHES, OVL, CAP, 2))(tile_patch_keys, tile_patch_turns).reshape((TILES, OVL))
    tile_offset = place_ends(jax.random.randint(key_list[3], (TILES, OVL, 2), 0, PS - TS + 1), jax.random.fold_in(key_list[3], 1), 0, PS - TS).astype(jnp.int32)
    coeffs = scatter_about(key_list[4], (EXPOSURES, NB), NB ** -0.5, 2.0, ((0, 32),))
    inv_var = jnp.clip(jnp.exp(math.log(4.0) - 2.7725887 * jax.random.uniform(key_list[5], (EXPOSURES,), jnp.float32) ** level_of(key_list[5], (EXPOSURES,), ((0, 32),), -0.2, 0.2)), 0.25, 4.0).astype(jnp.bfloat16)
    vert_taps = scatter_about(key_list[6], (NB, KW), KW ** -0.5, 1.0)
    horiz_taps = scatter_about(key_list[7], (NB, KW), KW ** -0.5, 1.0)
    return dict(tiles=tiles, tile_exposure=tile_exposure, tile_patch=tile_patch, tile_offset=tile_offset, coeffs=coeffs, inv_var=inv_var, vert_taps=vert_taps, horiz_taps=horiz_taps)


def band_matrix(filters, tile_side):
    terms, kernel_width = filters.shape
    half_width = (kernel_width - 1) // 2
    padding = tile_side - 1 - half_width
    padded = jnp.concatenate([jnp.zeros((terms, padding), jnp.float32), filters.astype(jnp.float32), jnp.zeros((terms, padding + 1), jnp.float32)], axis=1)
    tiled = jnp.tile(padded, (1, tile_side + 1))[:, : tile_side * (2 * tile_side + 1)]
    window = tiled.reshape(terms, tile_side, 2 * tile_side + 1)[:, :, :tile_side]
    return window[:, ::-1, :]


def reference(tiles, tile_exposure, tile_patch, tile_offset, coeffs, inv_var, vert_taps, horiz_taps):
    vband = band_matrix(vert_taps, TS)
    hband = band_matrix(horiz_taps, TS)
    coef_tile = coeffs[tile_exposure].astype(jnp.float32)
    weight_tile = inv_var[tile_exposure].astype(jnp.float32)
    groups = TILES // TILE_DEV
    block_tiles = tiles.reshape(groups, TILE_DEV, TS, TS)
    block_coef = coef_tile.reshape(groups, TILE_DEV, NB)
    block_weight = weight_tile.reshape(groups, TILE_DEV)
    block_patch = tile_patch.reshape(groups, TILE_DEV, OVL).astype(jnp.int32)
    block_offset = tile_offset.reshape(groups, TILE_DEV, OVL, 2).astype(jnp.int32)

    def one_block(carry, inputs):
        flux, cover = carry
        pixels, coef_rows, weights, patches, offsets = inputs
        rows_pass = jnp.einsum('tyk,bxk->tybx', pixels.astype(jnp.float32), hband, precision=lax.Precision.HIGHEST)
        partial_value = (rows_pass * coef_rows[:, None, :, None]).astype(jnp.bfloat16)
        smoothed = jnp.einsum('byk,tkbx->tyx', vband, partial_value.astype(jnp.float32), precision=lax.Precision.HIGHEST)
        weighted = (weights[:, None, None] * smoothed).astype(jnp.bfloat16)

        def add_entry(entry, inner):
            flux_in, cover_in = inner
            tile_pos = entry // OVL
            list_pos = entry % OVL
            patch = patches[tile_pos, list_pos].astype(jnp.int32)
            row_off = offsets[tile_pos, list_pos, 0].astype(jnp.int32)
            col_off = offsets[tile_pos, list_pos, 1].astype(jnp.int32)
            start = (patch, row_off, col_off)
            region = lax.dynamic_slice(flux_in, start, (1, TS, TS)) + weighted[tile_pos].astype(jnp.float32)[None]
            flux_in = lax.dynamic_update_slice(flux_in, region, start)
            spot = lax.dynamic_slice(cover_in, start, (1, TS, TS)) + weights[tile_pos]
            cover_in = lax.dynamic_update_slice(cover_in, spot, start)
            return (flux_in, cover_in)

        flux, cover = lax.fori_loop(0, TILE_DEV * OVL, add_entry, (flux, cover))
        return (flux, cover), None

    start_flux = jnp.zeros((PATCHES, PS, PS), jnp.float32)
    start_cover = jnp.zeros((PATCHES, PS, PS), jnp.float32)
    (flux, cover), _ = lax.scan(one_block, (start_flux, start_cover), (block_tiles, block_coef, block_weight, block_patch, block_offset))
    return flux / jnp.maximum(cover, 1.0)
```

```python
import functools

import jax
import jax.numpy as jnp
from jax import lax
from jax.experimental import pallas as pl
from jax.experimental.pallas import tpu as pltpu
from jax.sharding import PartitionSpec as P

PS = 512
MESH = pl.DeviceIdType.MESH
VMEM = pl.BlockSpec(memory_space=pltpu.VMEM)
SMEM = pl.BlockSpec(memory_space=pltpu.SMEM)


def gather_kernel(n_exp, n_grp, block_ref, out_ref, held, send_a, recv_a, send_b, recv_b):
    e = lax.axis_index("exp")
    g = lax.axis_index("grp")
    barrier = pltpu.get_barrier_semaphore()
    for i in range(1, n_grp):
        pl.semaphore_signal(
            barrier, inc=1, device_id=(e, lax.rem(g + i, n_grp)), device_id_type=MESH
        )
    for i in range(1, n_exp):
        pl.semaphore_signal(
            barrier, inc=1, device_id=(lax.rem(e + i, n_exp), g), device_id_type=MESH
        )
    pl.semaphore_wait(barrier, n_grp + n_exp - 2)

    held[e, g] = block_ref[...]
    copies = []
    for i in range(1, n_grp):
        copy = pltpu.make_async_remote_copy(
            src_ref=block_ref,
            dst_ref=held.at[e, g],
            send_sem=send_a.at[i - 1],
            recv_sem=recv_a.at[i - 1],
            device_id=(e, lax.rem(g + i, n_grp)),
            device_id_type=MESH,
        )
        copy.start()
        copies.append(copy)
    for copy in copies:
        copy.wait()
    copies = []
    for i in range(1, n_exp):
        copy = pltpu.make_async_remote_copy(
            src_ref=held.at[e],
            dst_ref=held.at[e],
            send_sem=send_b.at[i - 1],
            recv_sem=recv_b.at[i - 1],
            device_id=(lax.rem(e + i, n_exp), g),
            device_id_type=MESH,
        )
        copy.start()
        copies.append(copy)
    for copy in copies:
        copy.wait()
    out_ref[...] = held[...]


def gather_blocks(block, n_exp, n_grp):
    shape = (n_exp, n_grp) + block.shape
    return pl.pallas_call(
        functools.partial(gather_kernel, n_exp, n_grp),
        out_shape=jax.ShapeDtypeStruct(shape, block.dtype),
        in_specs=[VMEM],
        out_specs=VMEM,
        scratch_shapes=[
            pltpu.VMEM(shape, block.dtype),
            pltpu.SemaphoreType.DMA((n_grp - 1,)),
            pltpu.SemaphoreType.DMA((n_grp - 1,)),
            pltpu.SemaphoreType.DMA((n_exp - 1,)),
            pltpu.SemaphoreType.DMA((n_exp - 1,)),
        ],
        compiler_params=pltpu.CompilerParams(collective_id=0, has_side_effects=True),
    )(block)


def canvas_kernel(
    half, patch_ref, row_ref, col_ref, coef_ref, weight_ref, tiles_ref, vtap_ref, htap_ref,
    out_ref, vband, hband, weighted,
):
    terms, side = vtap_ref.shape
    count = tiles_ref.shape[0]
    listed = patch_ref.shape[0] // count
    patch = pl.program_id(0)

    @pl.when(patch == 0)
    def _():
        row = lax.broadcasted_iota(jnp.int32, (side, side), 0)
        col = lax.broadcasted_iota(jnp.int32, (side, side), 1)
        inside = jnp.abs(col - row) <= half

        def build(b, carry):
            for taps, band in ((vtap_ref, vband), (htap_ref, hband)):
                line = jnp.broadcast_to(taps[pl.ds(b, 1), :], (side, side))
                line = pltpu.roll(line, side - half // 8 * 8, 1, stride=1, stride_axis=0)
                band[b] = jnp.where(inside, line, 0.0).astype(jnp.bfloat16)
            return carry

        lax.fori_loop(0, terms, build, 0)

        def convolve(t, carry):
            tile = tiles_ref[t]
            total = jnp.zeros((side, side), jnp.float32)
            for b in range(terms):
                across = jnp.dot(tile, hband[b], preferred_element_type=jnp.float32)
                part = (across * coef_ref[t * terms + b]).astype(jnp.bfloat16)
                total += jnp.dot(vband[b], part, preferred_element_type=jnp.float32)
            weighted[t] = (weight_ref[t] * total).astype(jnp.bfloat16)
            return carry

        lax.fori_loop(0, count, convolve, 0)

    far = -4 * PS
    picked = [[jnp.int32(0), jnp.int32(far), jnp.int32(far)] for _ in range(2)]
    found = jnp.int32(0)
    for t in range(count):
        for j in range(listed):
            n = t * listed + j
            hit = patch_ref[n] == patch
            for slot in range(2):
                take = hit & (found == slot)
                picked[slot] = [
                    jnp.where(take, new, old)
                    for new, old in zip((t, row_ref[n], col_ref[n]), picked[slot])
                ]
            found = found + hit.astype(jnp.int32)

    inner_c = lax.broadcasted_iota(jnp.int32, (side, PS), 1) - lax.broadcasted_iota(
        jnp.int32, (side, PS), 0
    )
    inner_r = lax.broadcasted_iota(jnp.int32, (PS, side), 0) - lax.broadcasted_iota(
        jnp.int32, (PS, side), 1
    )
    canvas = jnp.zeros((PS, PS), jnp.float32)
    for t, row_off, col_off in picked:
        col_pick = jnp.where(inner_c == col_off, 1.0, 0.0).astype(jnp.bfloat16)
        row_pick = jnp.where(inner_r == row_off, 1.0, 0.0).astype(jnp.bfloat16)
        moved = jnp.dot(weighted[t], col_pick, preferred_element_type=jnp.float32)
        canvas += jnp.dot(
            row_pick, moved.astype(jnp.bfloat16), preferred_element_type=jnp.float32
        )
    out_ref[0] = canvas.astype(jnp.bfloat16)


def local_canvases(patches, tile_patch, tile_offset, coef_tile, weight_tile, tiles, vtaps, htaps):
    count, side, _ = tiles.shape
    terms, width = vtaps.shape
    half = (width - 1) // 2
    pad = ((0, 0), (0, side - width))
    vline = jnp.roll(jnp.pad(vtaps.astype(jnp.float32), pad), -(half % 8), axis=1)
    hline = jnp.roll(jnp.pad(htaps.astype(jnp.float32)[:, ::-1], pad), -(half % 8), axis=1)
    return pl.pallas_call(
        functools.partial(canvas_kernel, half),
        grid=(patches,),
        out_shape=jax.ShapeDtypeStruct((patches, PS, PS), jnp.bfloat16),
        in_specs=[SMEM] * 5 + [VMEM] * 3,
        out_specs=pl.BlockSpec((1, PS, PS), lambda p: (p, 0, 0)),
        scratch_shapes=[
            pltpu.VMEM((terms, side, side), jnp.bfloat16),
            pltpu.VMEM((terms, side, side), jnp.bfloat16),
            pltpu.VMEM((count, side, side), jnp.bfloat16),
        ],
        compiler_params=pltpu.CompilerParams(vmem_limit_bytes=40 << 20),
    )(
        tile_patch.reshape(-1),
        tile_offset[:, :, 0].reshape(-1),
        tile_offset[:, :, 1].reshape(-1),
        coef_tile.reshape(-1),
        weight_tile,
        tiles,
        vline,
        hline,
    )


def reduce_kernel(
    steps, canvas, out_ref, got1, sum1, got2, sum2, got3, sum3, got4, sends, recvs
):
    e = lax.axis_index("exp")
    g = lax.axis_index("grp")
    hi, lo = e // 2, lax.rem(e, 2)
    far, near = g // 2, lax.rem(g, 2)
    by_core = (e, 2 * far + 1 - near)
    by_x = (e, 2 * (1 - far) + near)
    by_y = (2 * hi + 1 - lo, g)
    goal = [lax.rem(hi + 1 + k, steps) for k in range(steps)]
    by_z = [(2 * goal[k] + lo, g) for k in range(steps - 1)]

    barrier = pltpu.get_barrier_semaphore()
    for partner in [by_core, by_x, by_y] + by_z:
        pl.semaphore_signal(barrier, inc=1, device_id=partner, device_id_type=MESH)
    pl.semaphore_wait(barrier, steps + 2)

    def send(stage, k, src, dst, partner):
        copy = pltpu.make_async_remote_copy(
            src_ref=src,
            dst_ref=dst,
            send_sem=sends.at[stage, k],
            recv_sem=recvs.at[stage, k],
            device_id=partner,
            device_id_type=MESH,
        )
        copy.start()
        return copy

    first = [
        send(0, k, canvas.at[pl.ds(2 * goal[k], 2), :, 1 - near], got1.at[k], by_core)
        for k in range(steps)
    ]
    second, third, fourth = [], [], []
    for k in range(steps):
        first[k].wait_recv()
        sum1[k] = canvas[pl.ds(2 * goal[k], 2), :, near] + got1[k]
        if k % 2 == 0:
            second.append(send(1, k, sum1.at[k, :, 1 - far], got2.at[k], by_x))
        else:
            second.append(send(1, k, sum1.at[k, 1 - lo], got2.at[k], by_y))
    for k in range(steps):
        second[k].wait_recv()
        if k % 2 == 0:
            sum2[k] = sum1[k, :, far] + got2[k]
            third.append(send(2, k, sum2.at[k, 1 - lo], got3.at[k], by_y))
        else:
            sum2[k] = sum1[k, lo] + got2[k]
            third.append(send(2, k, sum2.at[k, 1 - far], got3.at[k], by_x))
    for k in range(steps):
        third[k].wait_recv()
        own = sum2[k, lo] if k % 2 == 0 else sum2[k, far]
        if k < steps - 1:
            sum3[k] = own + got3[k]
            fourth.append(send(3, k, sum3.at[k], got4.at[k], by_z[k]))
        else:
            total = own.astype(jnp.float32) + got3[k].astype(jnp.float32)
    for k in range(steps - 1):
        fourth[k].wait_recv()
        total += got4[k].astype(jnp.float32)
    out_ref[...] = total
    for copy in first + second + third + fourth:
        copy.wait_send()


def reduce_canvases(canvases, n_exp, n_grp):
    rows = PS // n_grp
    if n_grp != 4 or n_exp % 2 or n_exp > 8:
        part = lax.psum_scatter(canvases, "exp", scatter_dimension=0, tiled=True)
        part = lax.psum_scatter(part, "grp", scatter_dimension=1, tiled=True)
        return part[0].astype(jnp.float32)
    steps = n_exp // 2
    kind = canvases.dtype
    return pl.pallas_call(
        functools.partial(reduce_kernel, steps),
        out_shape=jax.ShapeDtypeStruct((rows, PS), jnp.float32),
        in_specs=[VMEM],
        out_specs=VMEM,
        scratch_shapes=[
            pltpu.VMEM((steps, 2, 2, rows, PS), kind),
            pltpu.VMEM((steps, 2, 2, rows, PS), kind),
            pltpu.VMEM((steps, 2, rows, PS), kind),
            pltpu.VMEM((steps, 2, rows, PS), kind),
            pltpu.VMEM((steps, rows, PS), kind),
            pltpu.VMEM((steps - 1, rows, PS), kind),
            pltpu.VMEM((steps - 1, rows, PS), kind),
            pltpu.SemaphoreType.DMA((4, steps)),
            pltpu.SemaphoreType.DMA((4, steps)),
        ],
        compiler_params=pltpu.CompilerParams(
            collective_id=1, has_side_effects=True, vmem_limit_bytes=40 << 20
        ),
    )(canvases.reshape(n_exp, 2, 2, rows, PS))


def per_device(
    tiles, tile_exposure, tile_patch, tile_offset, coeffs, inv_var, vert_taps, horiz_taps
):
    n_exp = lax.axis_size("exp")
    n_grp = lax.axis_size("grp")
    count, side, _ = tiles.shape
    listed = tile_patch.shape[1]
    held, terms = coeffs.shape
    f32 = jnp.float32
    top = jnp.concatenate([coeffs, inv_var[:, None]], axis=1).astype(f32)
    low = jnp.concatenate(
        [tile_exposure[:, None], tile_patch, tile_offset[:, :, 0], tile_offset[:, :, 1]], axis=1
    ).astype(f32)
    lines = -(-(held + count) // 8) * 8
    block = jnp.concatenate(
        [
            jnp.pad(top, ((0, 0), (0, 128 - top.shape[1]))),
            jnp.pad(low, ((0, lines - held - count), (0, 128 - low.shape[1]))),
        ],
        axis=0,
    )
    every = gather_blocks(block, n_exp, n_grp).reshape(n_exp * n_grp, lines, 128)
    table = every[:, :held, : terms + 1].reshape(-1, terms + 1).astype(jnp.bfloat16)
    tags = every[:, held : held + count, : low.shape[1]].reshape(-1, low.shape[1])
    names = tags[:, 0].astype(jnp.int32)
    exposures = jnp.arange(table.shape[0], dtype=jnp.int32)
    mine = jnp.dot(
        (tile_exposure[:, None] == exposures[None, :]).astype(jnp.bfloat16),
        table,
        preferred_element_type=f32,
    )
    canvases = local_canvases(
        n_exp, tile_patch, tile_offset, mine[:, :terms], mine[:, terms], tiles, vert_taps, horiz_taps
    )

    weights = jnp.dot(
        (names[:, None] == exposures[None, :]).astype(jnp.bfloat16),
        table[:, terms:],
        preferred_element_type=f32,
    )
    here = (tags[:, 1 : 1 + listed] == lax.axis_index("exp").astype(f32)).astype(f32)
    named = jnp.sum(here, axis=1, keepdims=True) > 0
    row_off = jnp.sum(here * tags[:, 1 + listed : 1 + 2 * listed], axis=1, keepdims=True)
    col_off = jnp.sum(here * tags[:, 1 + 2 * listed : 1 + 3 * listed], axis=1, keepdims=True)
    rows = PS // n_grp
    y = (jnp.arange(rows, dtype=jnp.int32) + lax.axis_index("grp") * rows).astype(f32)[None, :]
    x = jnp.arange(PS, dtype=jnp.int32).astype(f32)[None, :]
    row_mask = jnp.where(named & (y >= row_off) & (y < row_off + side), weights, 0.0)
    col_mask = (x >= col_off) & (x < col_off + side)
    cover = lax.dot_general(
        row_mask.astype(jnp.bfloat16),
        col_mask.astype(jnp.bfloat16),
        (((0,), (0,)), ((), ())),
        preferred_element_type=f32,
    )
    flux = reduce_canvases(canvases, n_exp, n_grp)
    return (flux / jnp.maximum(cover, 1.0))[None]


def solution(mesh):
    in_specs = (
        P(("exp", "grp"), None, None),
        P(("exp", "grp")),
        P(("exp", "grp"), None),
        P(("exp", "grp"), None, None),
        P(("exp", "grp"), None),
        P(("exp", "grp")),
        P(),
        P(),
    )
    out_specs = P("exp", "grp", None)
    return jax.shard_map(
        per_device, mesh=mesh, in_specs=in_specs, out_specs=out_specs, check_vma=False
    )
```

```python
import functools

import jax
import jax.numpy as jnp
from jax import lax
from jax.experimental import pallas as pl
from jax.experimental.pallas import tpu as pltpu
from jax.sharding import PartitionSpec as P

PS = 512
MESH = pl.DeviceIdType.MESH
VMEM = pl.BlockSpec(memory_space=pltpu.VMEM)
SMEM = pl.BlockSpec(memory_space=pltpu.SMEM)


def gather_kernel(n_exp, n_grp, block_ref, out_ref, held, send_a, recv_a, send_b, recv_b):
    e = lax.axis_index("exp")
    g = lax.axis_index("grp")
    barrier = pltpu.get_barrier_semaphore()
    for i in range(1, n_grp):
        pl.semaphore_signal(
            barrier, inc=1, device_id=(e, lax.rem(g + i, n_grp)), device_id_type=MESH
        )
    for i in range(1, n_exp):
        pl.semaphore_signal(
            barrier, inc=1, device_id=(lax.rem(e + i, n_exp), g), device_id_type=MESH
        )
    pl.semaphore_wait(barrier, n_grp + n_exp - 2)

    held[e, g] = block_ref[...]
    copies = []
    for i in range(1, n_grp):
        copy = pltpu.make_async_remote_copy(
            src_ref=block_ref,
            dst_ref=held.at[e, g],
            send_sem=send_a.at[i - 1],
            recv_sem=recv_a.at[i - 1],
            device_id=(e, lax.rem(g + i, n_grp)),
            device_id_type=MESH,
        )
        copy.start()
        copies.append(copy)
    for copy in copies:
        copy.wait()
    copies = []
    for i in range(1, n_exp):
        copy = pltpu.make_async_remote_copy(
            src_ref=held.at[e],
            dst_ref=held.at[e],
            send_sem=send_b.at[i - 1],
            recv_sem=recv_b.at[i - 1],
            device_id=(lax.rem(e + i, n_exp), g),
            device_id_type=MESH,
        )
        copy.start()
        copies.append(copy)
    for copy in copies:
        copy.wait()
    out_ref[...] = held[...]


def gather_blocks(block, n_exp, n_grp):
    shape = (n_exp, n_grp) + block.shape
    return pl.pallas_call(
        functools.partial(gather_kernel, n_exp, n_grp),
        out_shape=jax.ShapeDtypeStruct(shape, block.dtype),
        in_specs=[VMEM],
        out_specs=VMEM,
        scratch_shapes=[
            pltpu.VMEM(shape, block.dtype),
            pltpu.SemaphoreType.DMA((n_grp - 1,)),
            pltpu.SemaphoreType.DMA((n_grp - 1,)),
            pltpu.SemaphoreType.DMA((n_exp - 1,)),
            pltpu.SemaphoreType.DMA((n_exp - 1,)),
        ],
        compiler_params=pltpu.CompilerParams(collective_id=0, has_side_effects=True),
    )(block)


def canvas_kernel(
    half, patch_ref, row_ref, col_ref, coef_ref, weight_ref, tiles_ref, vtap_ref, htap_ref,
    out_ref, vband, hband, weighted,
):
    terms, side = vtap_ref.shape
    count = tiles_ref.shape[0]
    listed = patch_ref.shape[0] // count
    patch = pl.program_id(0)

    @pl.when(patch == 0)
    def _():
        row = lax.broadcasted_iota(jnp.int32, (side, side), 0)
        col = lax.broadcasted_iota(jnp.int32, (side, side), 1)
        inside = jnp.abs(col - row) <= half

        def build(b, carry):
            for taps, band in ((vtap_ref, vband), (htap_ref, hband)):
                line = jnp.broadcast_to(taps[pl.ds(b, 1), :], (side, side))
                line = pltpu.roll(line, side - half // 8 * 8, 1, stride=1, stride_axis=0)
                band[b] = jnp.where(inside, line, 0.0).astype(jnp.bfloat16)
            return carry

        lax.fori_loop(0, terms, build, 0)

        def convolve(t, carry):
            tile = tiles_ref[t]
            total = jnp.zeros((side, side), jnp.float32)
            for b in range(terms):
                across = jnp.dot(tile, hband[b], preferred_element_type=jnp.float32)
                part = (across * coef_ref[t * terms + b]).astype(jnp.bfloat16)
                total += jnp.dot(vband[b], part, preferred_element_type=jnp.float32)
            weighted[t] = (weight_ref[t] * total).astype(jnp.bfloat16)
            return carry

        lax.fori_loop(0, count, convolve, 0)

    far = -4 * PS
    picked = [[jnp.int32(0), jnp.int32(far), jnp.int32(far)] for _ in range(2)]
    found = jnp.int32(0)
    for t in range(count):
        for j in range(listed):
            n = t * listed + j
            hit = patch_ref[n] == patch
            for slot in range(2):
                take = hit & (found == slot)
                picked[slot] = [
                    jnp.where(take, new, old)
                    for new, old in zip((t, row_ref[n], col_ref[n]), picked[slot])
                ]
            found = found + hit.astype(jnp.int32)

    inner_c = lax.broadcasted_iota(jnp.int32, (side, PS), 1) - lax.broadcasted_iota(
        jnp.int32, (side, PS), 0
    )
    inner_r = lax.broadcasted_iota(jnp.int32, (PS, side), 0) - lax.broadcasted_iota(
        jnp.int32, (PS, side), 1
    )
    canvas = jnp.zeros((PS, PS), jnp.float32)
    for t, row_off, col_off in picked:
        col_pick = jnp.where(inner_c == col_off, 1.0, 0.0).astype(jnp.bfloat16)
        row_pick = jnp.where(inner_r == row_off, 1.0, 0.0).astype(jnp.bfloat16)
        moved = jnp.dot(weighted[t], col_pick, preferred_element_type=jnp.float32)
        canvas += jnp.dot(
            row_pick, moved.astype(jnp.bfloat16), preferred_element_type=jnp.float32
        )
    out_ref[0] = canvas.astype(jnp.bfloat16)


def local_canvases(patches, tile_patch, tile_offset, coef_tile, weight_tile, tiles, vtaps, htaps):
    count, side, _ = tiles.shape
    terms, width = vtaps.shape
    half = (width - 1) // 2
    pad = ((0, 0), (0, side - width))
    vline = jnp.roll(jnp.pad(vtaps.astype(jnp.float32), pad), -(half % 8), axis=1)
    hline = jnp.roll(jnp.pad(htaps.astype(jnp.float32)[:, ::-1], pad), -(half % 8), axis=1)
    return pl.pallas_call(
        functools.partial(canvas_kernel, half),
        grid=(patches,),
        out_shape=jax.ShapeDtypeStruct((patches, PS, PS), jnp.bfloat16),
        in_specs=[SMEM] * 5 + [VMEM] * 3,
        out_specs=pl.BlockSpec((1, PS, PS), lambda p: (p, 0, 0)),
        scratch_shapes=[
            pltpu.VMEM((terms, side, side), jnp.bfloat16),
            pltpu.VMEM((terms, side, side), jnp.bfloat16),
            pltpu.VMEM((count, side, side), jnp.bfloat16),
        ],
        compiler_params=pltpu.CompilerParams(vmem_limit_bytes=40 << 20),
    )(
        tile_patch.reshape(-1),
        tile_offset[:, :, 0].reshape(-1),
        tile_offset[:, :, 1].reshape(-1),
        coef_tile.reshape(-1),
        weight_tile,
        tiles,
        vline,
        hline,
    )


def reduce_kernel(
    steps, canvas, out_ref, got1, sum1, got2, sum2, got3, sum3, got4, sends, recvs
):
    e = lax.axis_index("exp")
    g = lax.axis_index("grp")
    hi, lo = e // 2, lax.rem(e, 2)
    far, near = g // 2, lax.rem(g, 2)
    by_core = (e, 2 * far + 1 - near)
    by_x = (e, 2 * (1 - far) + near)
    by_y = (2 * hi + 1 - lo, g)
    goal = [lax.rem(hi + 1 + k, steps) for k in range(steps)]
    by_z = [(2 * goal[k] + lo, g) for k in range(steps - 1)]

    barrier = pltpu.get_barrier_semaphore()
    for partner in [by_core, by_x, by_y] + by_z:
        pl.semaphore_signal(barrier, inc=1, device_id=partner, device_id_type=MESH)
    pl.semaphore_wait(barrier, steps + 2)

    def send(stage, k, src, dst, partner):
        copy = pltpu.make_async_remote_copy(
            src_ref=src,
            dst_ref=dst,
            send_sem=sends.at[stage, k],
            recv_sem=recvs.at[stage, k],
            device_id=partner,
            device_id_type=MESH,
        )
        copy.start()
        return copy

    first = [
        send(0, k, canvas.at[pl.ds(2 * goal[k], 2), :, 1 - near], got1.at[k], by_core)
        for k in range(steps)
    ]
    second, third, fourth = [], [], []
    for k in range(steps):
        first[k].wait_recv()
        sum1[k] = canvas[pl.ds(2 * goal[k], 2), :, near] + got1[k]
        if k % 2 == 0:
            second.append(send(1, k, sum1.at[k, :, 1 - far], got2.at[k], by_x))
        else:
            second.append(send(1, k, sum1.at[k, 1 - lo], got2.at[k], by_y))
    for k in range(steps):
        second[k].wait_recv()
        if k % 2 == 0:
            sum2[k] = sum1[k, :, far] + got2[k]
            third.append(send(2, k, sum2.at[k, 1 - lo], got3.at[k], by_y))
        else:
            sum2[k] = sum1[k, lo] + got2[k]
            third.append(send(2, k, sum2.at[k, 1 - far], got3.at[k], by_x))
    for k in range(steps):
        third[k].wait_recv()
        own = sum2[k, lo] if k % 2 == 0 else sum2[k, far]
        if k < steps - 1:
            sum3[k] = own + got3[k]
            fourth.append(send(3, k, sum3.at[k], got4.at[k], by_z[k]))
        else:
            total = own.astype(jnp.float32) + got3[k].astype(jnp.float32)
    for k in range(steps - 1):
        fourth[k].wait_recv()
        total += got4[k].astype(jnp.float32)
    out_ref[...] = total
    for copy in first + second + third + fourth:
        copy.wait_send()


def reduce_canvases(canvases, n_exp, n_grp):
    rows = PS // n_grp
    if n_grp != 4 or n_exp % 2 or n_exp > 8:
        part = lax.psum_scatter(canvases, "exp", scatter_dimension=0, tiled=True)
        part = lax.psum_scatter(part, "grp", scatter_dimension=1, tiled=True)
        return part[0].astype(jnp.float32)
    steps = n_exp // 2
    kind = canvases.dtype
    return pl.pallas_call(
        functools.partial(reduce_kernel, steps),
        out_shape=jax.ShapeDtypeStruct((rows, PS), jnp.float32),
        in_specs=[VMEM],
        out_specs=VMEM,
        scratch_shapes=[
            pltpu.VMEM((steps, 2, 2, rows, PS), kind),
            pltpu.VMEM((steps, 2, 2, rows, PS), kind),
            pltpu.VMEM((steps, 2, rows, PS), kind),
            pltpu.VMEM((steps, 2, rows, PS), kind),
            pltpu.VMEM((steps, rows, PS), kind),
            pltpu.VMEM((steps - 1, rows, PS), kind),
            pltpu.VMEM((steps - 1, rows, PS), kind),
            pltpu.SemaphoreType.DMA((4, steps)),
            pltpu.SemaphoreType.DMA((4, steps)),
        ],
        compiler_params=pltpu.CompilerParams(
            collective_id=1, has_side_effects=True, vmem_limit_bytes=40 << 20
        ),
    )(canvases.reshape(n_exp, 2, 2, rows, PS))


def fused_kernel(
    shape, exposure_ref, patch_ref, offset_ref, top_ref, tiles_ref, taps_ref, out_ref,
    block, held, vband, hband, weighted, canvas, got1, sum1, got2, sum2, got3, sum3, got4,
    send_a, recv_a, send_b, recv_b, sends, recvs,
):
    n_exp, n_grp, own_rows, half = shape
    steps = n_exp // 2
    terms = vband.shape[0]
    count, side, _ = tiles_ref.shape
    listed = patch_ref.shape[1]
    rows = PS // n_grp
    lines = block.shape[0]
    f32, i32, bf16 = jnp.float32, jnp.int32, jnp.bfloat16
    e = lax.axis_index("exp")
    g = lax.axis_index("grp")
    hi, lo = e // 2, lax.rem(e, 2)
    far, near = g // 2, lax.rem(g, 2)
    by_core = (e, 2 * far + 1 - near)
    by_x = (e, 2 * (1 - far) + near)
    by_y = (2 * hi + 1 - lo, g)
    goal = [lax.rem(hi + 1 + k, steps) for k in range(steps)]
    by_z = [(2 * goal[k] + lo, g) for k in range(steps - 1)]
    by_grp = [(e, lax.rem(g + i, n_grp)) for i in range(1, n_grp)]
    by_exp = [(lax.rem(e + i, n_exp), g) for i in range(1, n_exp)]

    barrier = pltpu.get_barrier_semaphore()
    for partner in by_grp + by_exp:
        pl.semaphore_signal(barrier, inc=1, device_id=partner, device_id_type=MESH)

    line = lax.broadcasted_iota(i32, (lines, 128), 0)
    lane = lax.broadcasted_iota(i32, (lines, 128), 1)
    data = top_ref[...]
    for t in range(count):
        values = [exposure_ref[t]] + [patch_ref[t, j] for j in range(listed)]
        values += [offset_ref[t, 2 * j + c] for c in range(2) for j in range(listed)]
        for n, value in enumerate(values):
            data = jnp.where((line == own_rows + t) & (lane == n), value.astype(f32), data)
    block[...] = data
    held[e, g] = data

    pl.semaphore_wait(barrier, n_grp + n_exp - 2)

    def copy_to(src, dst, send_sem, recv_sem, partner):
        copy = pltpu.make_async_remote_copy(
            src_ref=src, dst_ref=dst, send_sem=send_sem, recv_sem=recv_sem,
            device_id=partner, device_id_type=MESH,
        )
        copy.start()
        return copy

    row = lax.broadcasted_iota(i32, (side, side), 0)
    col = lax.broadcasted_iota(i32, (side, side), 1)
    inside = jnp.abs(col - row) <= half

    def build(band, base):
        def one(b, carry):
            taps = jnp.broadcast_to(taps_ref[pl.ds(base + b, 1), :], (side, side))
            taps = pltpu.roll(taps, side - half // 8 * 8, 1, stride=1, stride_axis=0)
            band[b] = jnp.where(inside, taps, 0.0).astype(bf16)
            return carry

        lax.fori_loop(0, terms, one, 0)

    copies = [
        copy_to(block, held.at[e, g], send_a.at[i], recv_a.at[i], partner)
        for i, partner in enumerate(by_grp)
    ]
    build(hband, terms)
    for copy in copies:
        copy.wait()
    copies = [
        copy_to(held.at[e], held.at[e], send_b.at[i], recv_b.at[i], partner)
        for i, partner in enumerate(by_exp)
    ]
    build(vband, 0)
    for copy in copies:
        copy.wait()

    every = held[...].reshape(n_exp * n_grp * lines, 128)
    total_lines = n_exp * n_grp * lines
    spot = lax.broadcasted_iota(i32, (total_lines, 128), 0)
    number = jnp.where(spot % lines < own_rows, spot // lines * own_rows + spot % lines, -1)

    def convolve(t, carry):
        mine = jnp.sum(jnp.where(number == exposure_ref[t], every, 0.0), axis=0, keepdims=True)
        tile = tiles_ref[t]
        total = jnp.zeros((side, side), f32)
        for b in range(terms):
            across = jnp.dot(tile, hband[b], preferred_element_type=f32)
            part = (across * mine[:, b : b + 1]).astype(bf16)
            total += jnp.dot(vband[b], part, preferred_element_type=f32)
        weighted[t] = (mine[:, terms : terms + 1] * total).astype(bf16)
        return carry

    lax.fori_loop(0, count, convolve, 0)

    inner_c = lax.broadcasted_iota(i32, (side, PS), 1) - lax.broadcasted_iota(i32, (side, PS), 0)
    inner_r = lax.broadcasted_iota(i32, (PS, side), 0) - lax.broadcasted_iota(i32, (PS, side), 1)

    def place(k):
        def one(y, carry):
            patch = 2 * goal[k] + y
            picked = [[i32(0), i32(-4 * PS), i32(-4 * PS)] for _ in range(2)]
            found = i32(0)
            for t in range(count):
                for j in range(listed):
                    hit = patch_ref[t, j] == patch
                    new = (i32(t), offset_ref[t, 2 * j], offset_ref[t, 2 * j + 1])
                    for slot in range(2):
                        take = hit & (found == slot)
                        picked[slot] = [
                            jnp.where(take, a, b) for a, b in zip(new, picked[slot])
                        ]
                    found = found + jnp.where(hit, 1, 0)
            image = jnp.zeros((PS, PS), f32)
            for t, row_off, col_off in picked:
                col_pick = jnp.where(inner_c == col_off, 1.0, 0.0).astype(bf16)
                row_pick = jnp.where(inner_r == row_off, 1.0, 0.0).astype(bf16)
                moved = jnp.dot(weighted[t], col_pick, preferred_element_type=f32)
                image += jnp.dot(row_pick, moved.astype(bf16), preferred_element_type=f32)
            canvas[k, y] = image.astype(bf16).reshape(2, 2, rows, PS)
            return carry

        lax.fori_loop(0, 2, one, 0)

    def send(stage, k, src, dst, partner):
        return copy_to(src, dst, sends.at[stage, k], recvs.at[stage, k], partner)

    first, second, third, fourth = [], [], [], []

    def second_step(k):
        first[k].wait_recv()
        sum1[k] = canvas[k, :, :, near] + got1[k]
        if k % 2 == 0:
            second.append(send(1, k, sum1.at[k, :, 1 - far], got2.at[k], by_x))
        else:
            second.append(send(1, k, sum1.at[k, 1 - lo], got2.at[k], by_y))

    for k in range(steps):
        place(k)
        first.append(send(0, k, canvas.at[k, :, :, 1 - near], got1.at[k], by_core))
        if k > 0:
            second_step(k - 1)
    second_step(steps - 1)

    tag = lambda n: every[:, n : n + 1]
    row_off = jnp.full((total_lines, 1), -4.0 * PS, f32)
    col_off = row_off
    for j in range(listed):
        hit = tag(1 + j) == e.astype(f32)
        row_off = jnp.where(hit, tag(1 + listed + j), row_off)
        col_off = jnp.where(hit, tag(1 + 2 * listed + j), col_off)
    down = lax.broadcasted_iota(i32, (total_lines, total_lines), 1)
    down = jnp.where(down % lines < own_rows, down // lines * own_rows + down % lines, -1)
    chosen = jnp.where(tag(0) == down.astype(f32), 1.0, 0.0).astype(bf16)
    weights = jnp.dot(chosen, every.astype(bf16), preferred_element_type=f32)
    weights = weights[:, terms : terms + 1]
    kept = lax.broadcasted_iota(i32, (total_lines, 1), 0) % lines
    weights = jnp.where((kept >= own_rows) & (kept < own_rows + count), weights, 0.0)
    y = (lax.broadcasted_iota(i32, (total_lines, rows), 1) + g * rows).astype(f32)
    x = lax.broadcasted_iota(i32, (total_lines, PS), 1).astype(f32)
    row_mask = jnp.where((y >= row_off) & (y < row_off + side), weights, 0.0).astype(bf16)
    col_mask = jnp.where((x >= col_off) & (x < col_off + side), 1.0, 0.0).astype(bf16)
    cover = lax.dot_general(
        row_mask, col_mask, (((0,), (0,)), ((), ())), preferred_element_type=f32
    )
    out_ref[0] = jnp.maximum(cover, 1.0)

    for k in range(steps):
        second[k].wait_recv()
        if k % 2 == 0:
            sum2[k] = sum1[k, :, far] + got2[k]
            third.append(send(2, k, sum2.at[k, 1 - lo], got3.at[k], by_y))
        else:
            sum2[k] = sum1[k, lo] + got2[k]
            third.append(send(2, k, sum2.at[k, 1 - far], got3.at[k], by_x))
    for k in range(steps):
        third[k].wait_recv()
        own = sum2[k, lo] if k % 2 == 0 else sum2[k, far]
        if k < steps - 1:
            sum3[k] = own + got3[k]
            fourth.append(send(3, k, sum3.at[k], got4.at[k], by_z[k]))
        else:
            total = own.astype(f32) + got3[k].astype(f32)
    for k in range(steps - 1):
        fourth[k].wait_recv()
        total += got4[k].astype(f32)
    out_ref[0] = total / out_ref[0]
    for copy in first + second + third + fourth:
        copy.wait_send()


def fused(
    n_exp, n_grp, tiles, tile_exposure, tile_patch, tile_offset, coeffs, inv_var, vtaps, htaps
):
    count, side, _ = tiles.shape
    terms, width = vtaps.shape
    half = (width - 1) // 2
    own_rows = coeffs.shape[0]
    lines = -(-(own_rows + count) // 8) * 8
    rows = PS // n_grp
    steps = n_exp // 2
    f32, kind = jnp.float32, jnp.bfloat16
    top = jnp.concatenate([coeffs, inv_var[:, None]], axis=1).astype(f32)
    top = jnp.pad(top, ((0, lines - own_rows), (0, 128 - terms - 1)))
    taps = jnp.concatenate([vtaps, htaps[:, ::-1]], axis=0).astype(f32)
    taps = jnp.concatenate(
        [
            taps[:, half % 8 :],
            jnp.zeros((2 * terms, side - width), f32),
            taps[:, : half % 8],
        ],
        axis=1,
    )
    dma = pltpu.SemaphoreType.DMA
    return pl.pallas_call(
        functools.partial(fused_kernel, (n_exp, n_grp, own_rows, half)),
        out_shape=jax.ShapeDtypeStruct((1, rows, PS), f32),
        in_specs=[SMEM] * 3 + [VMEM] * 3,
        out_specs=VMEM,
        scratch_shapes=[
            pltpu.VMEM((lines, 128), f32),
            pltpu.VMEM((n_exp, n_grp, lines, 128), f32),
            pltpu.VMEM((terms, side, side), kind),
            pltpu.VMEM((terms, side, side), kind),
            pltpu.VMEM((count, side, side), kind),
            pltpu.VMEM((steps, 2, 2, 2, rows, PS), kind),
            pltpu.VMEM((steps, 2, 2, rows, PS), kind),
            pltpu.VMEM((steps, 2, 2, rows, PS), kind),
            pltpu.VMEM((steps, 2, rows, PS), kind),
            pltpu.VMEM((steps, 2, rows, PS), kind),
            pltpu.VMEM((steps, rows, PS), kind),
            pltpu.VMEM((steps - 1, rows, PS), kind),
            pltpu.VMEM((steps - 1, rows, PS), kind),
            dma((n_grp - 1,)),
            dma((n_grp - 1,)),
            dma((n_exp - 1,)),
            dma((n_exp - 1,)),
            dma((4, steps)),
            dma((4, steps)),
        ],
        compiler_params=pltpu.CompilerParams(
            collective_id=2, has_side_effects=True, vmem_limit_bytes=48 << 20
        ),
    )(tile_exposure, tile_patch, tile_offset.reshape(count, -1), top, tiles, taps)


def per_device(
    tiles, tile_exposure, tile_patch, tile_offset, coeffs, inv_var, vert_taps, horiz_taps
):
    n_exp = lax.axis_size("exp")
    n_grp = lax.axis_size("grp")
    count, side, _ = tiles.shape
    listed = tile_patch.shape[1]
    held, terms = coeffs.shape
    f32 = jnp.float32
    if n_grp == 4 and n_exp % 2 == 0 and 4 <= n_exp <= 8:
        return fused(
            n_exp, n_grp, tiles, tile_exposure, tile_patch, tile_offset, coeffs, inv_var,
            vert_taps, horiz_taps,
        )
    top = jnp.concatenate([coeffs, inv_var[:, None]], axis=1).astype(f32)
    low = jnp.concatenate(
        [tile_exposure[:, None], tile_patch, tile_offset[:, :, 0], tile_offset[:, :, 1]], axis=1
    ).astype(f32)
    lines = -(-(held + count) // 8) * 8
    block = jnp.concatenate(
        [
            jnp.pad(top, ((0, 0), (0, 128 - top.shape[1]))),
            jnp.pad(low, ((0, lines - held - count), (0, 128 - low.shape[1]))),
        ],
        axis=0,
    )
    every = gather_blocks(block, n_exp, n_grp).reshape(n_exp * n_grp, lines, 128)
    table = every[:, :held, : terms + 1].reshape(-1, terms + 1).astype(jnp.bfloat16)
    tags = every[:, held : held + count, : low.shape[1]].reshape(-1, low.shape[1])
    names = tags[:, 0].astype(jnp.int32)
    exposures = jnp.arange(table.shape[0], dtype=jnp.int32)
    mine = jnp.dot(
        (tile_exposure[:, None] == exposures[None, :]).astype(jnp.bfloat16),
        table,
        preferred_element_type=f32,
    )
    canvases = local_canvases(
        n_exp, tile_patch, tile_offset, mine[:, :terms], mine[:, terms], tiles, vert_taps, horiz_taps
    )

    weights = jnp.dot(
        (names[:, None] == exposures[None, :]).astype(jnp.bfloat16),
        table[:, terms:],
        preferred_element_type=f32,
    )
    here = (tags[:, 1 : 1 + listed] == lax.axis_index("exp").astype(f32)).astype(f32)
    named = jnp.sum(here, axis=1, keepdims=True) > 0
    row_off = jnp.sum(here * tags[:, 1 + listed : 1 + 2 * listed], axis=1, keepdims=True)
    col_off = jnp.sum(here * tags[:, 1 + 2 * listed : 1 + 3 * listed], axis=1, keepdims=True)
    rows = PS // n_grp
    y = (jnp.arange(rows, dtype=jnp.int32) + lax.axis_index("grp") * rows).astype(f32)[None, :]
    x = jnp.arange(PS, dtype=jnp.int32).astype(f32)[None, :]
    row_mask = jnp.where(named & (y >= row_off) & (y < row_off + side), weights, 0.0)
    col_mask = (x >= col_off) & (x < col_off + side)
    cover = lax.dot_general(
        row_mask.astype(jnp.bfloat16),
        col_mask.astype(jnp.bfloat16),
        (((0,), (0,)), ((), ())),
        preferred_element_type=f32,
    )
    flux = reduce_canvases(canvases, n_exp, n_grp)
    return (flux / jnp.maximum(cover, 1.0))[None]


def solution(mesh):
    in_specs = (
        P(("exp", "grp"), None, None),
        P(("exp", "grp")),
        P(("exp", "grp"), None),
        P(("exp", "grp"), None, None),
        P(("exp", "grp"), None),
        P(("exp", "grp")),
        P(),
        P(),
    )
    out_specs = P("exp", "grp", None)
    return jax.shard_map(
        per_device, mesh=mesh, in_specs=in_specs, out_specs=out_specs, check_vma=False
    )
```

```python
import functools

import jax
import jax.numpy as jnp
from jax import lax
from jax.experimental import pallas as pl
from jax.experimental.pallas import tpu as pltpu
from jax.sharding import PartitionSpec as P

PS = 512
MESH = pl.DeviceIdType.MESH
VMEM = pl.BlockSpec(memory_space=pltpu.VMEM)
SMEM = pl.BlockSpec(memory_space=pltpu.SMEM)


def gather_kernel(n_exp, n_grp, block_ref, out_ref, held, send_a, recv_a, send_b, recv_b):
    e = lax.axis_index("exp")
    g = lax.axis_index("grp")
    barrier = pltpu.get_barrier_semaphore()
    for i in range(1, n_grp):
        pl.semaphore_signal(
            barrier, inc=1, device_id=(e, lax.rem(g + i, n_grp)), device_id_type=MESH
        )
    for i in range(1, n_exp):
        pl.semaphore_signal(
            barrier, inc=1, device_id=(lax.rem(e + i, n_exp), g), device_id_type=MESH
        )
    pl.semaphore_wait(barrier, n_grp + n_exp - 2)

    held[e, g] = block_ref[...]
    copies = []
    for i in range(1, n_grp):
        copy = pltpu.make_async_remote_copy(
            src_ref=block_ref,
            dst_ref=held.at[e, g],
            send_sem=send_a.at[i - 1],
            recv_sem=recv_a.at[i - 1],
            device_id=(e, lax.rem(g + i, n_grp)),
            device_id_type=MESH,
        )
        copy.start()
        copies.append(copy)
    for copy in copies:
        copy.wait()
    copies = []
    for i in range(1, n_exp):
        copy = pltpu.make_async_remote_copy(
            src_ref=held.at[e],
            dst_ref=held.at[e],
            send_sem=send_b.at[i - 1],
            recv_sem=recv_b.at[i - 1],
            device_id=(lax.rem(e + i, n_exp), g),
            device_id_type=MESH,
        )
        copy.start()
        copies.append(copy)
    for copy in copies:
        copy.wait()
    out_ref[...] = held[...]


def gather_blocks(block, n_exp, n_grp):
    shape = (n_exp, n_grp) + block.shape
    return pl.pallas_call(
        functools.partial(gather_kernel, n_exp, n_grp),
        out_shape=jax.ShapeDtypeStruct(shape, block.dtype),
        in_specs=[VMEM],
        out_specs=VMEM,
        scratch_shapes=[
            pltpu.VMEM(shape, block.dtype),
            pltpu.SemaphoreType.DMA((n_grp - 1,)),
            pltpu.SemaphoreType.DMA((n_grp - 1,)),
            pltpu.SemaphoreType.DMA((n_exp - 1,)),
            pltpu.SemaphoreType.DMA((n_exp - 1,)),
        ],
        compiler_params=pltpu.CompilerParams(collective_id=0, has_side_effects=True),
    )(block)


def canvas_kernel(
    half, patch_ref, row_ref, col_ref, coef_ref, weight_ref, tiles_ref, vtap_ref, htap_ref,
    out_ref, vband, hband, weighted,
):
    terms, side = vtap_ref.shape
    count = tiles_ref.shape[0]
    listed = patch_ref.shape[0] // count
    patch = pl.program_id(0)

    @pl.when(patch == 0)
    def _():
        row = lax.broadcasted_iota(jnp.int32, (side, side), 0)
        col = lax.broadcasted_iota(jnp.int32, (side, side), 1)
        inside = jnp.abs(col - row) <= half

        def build(b, carry):
            for taps, band in ((vtap_ref, vband), (htap_ref, hband)):
                line = jnp.broadcast_to(taps[pl.ds(b, 1), :], (side, side))
                line = pltpu.roll(line, side - half // 8 * 8, 1, stride=1, stride_axis=0)
                band[b] = jnp.where(inside, line, 0.0).astype(jnp.bfloat16)
            return carry

        lax.fori_loop(0, terms, build, 0)

        def convolve(t, carry):
            tile = tiles_ref[t]
            total = jnp.zeros((side, side), jnp.float32)
            for b in range(terms):
                across = jnp.dot(tile, hband[b], preferred_element_type=jnp.float32)
                part = (across * coef_ref[t * terms + b]).astype(jnp.bfloat16)
                total += jnp.dot(vband[b], part, preferred_element_type=jnp.float32)
            weighted[t] = (weight_ref[t] * total).astype(jnp.bfloat16)
            return carry

        lax.fori_loop(0, count, convolve, 0)

    far = -4 * PS
    picked = [[jnp.int32(0), jnp.int32(far), jnp.int32(far)] for _ in range(2)]
    found = jnp.int32(0)
    for t in range(count):
        for j in range(listed):
            n = t * listed + j
            hit = patch_ref[n] == patch
            for slot in range(2):
                take = hit & (found == slot)
                picked[slot] = [
                    jnp.where(take, new, old)
                    for new, old in zip((t, row_ref[n], col_ref[n]), picked[slot])
                ]
            found = found + hit.astype(jnp.int32)

    inner_c = lax.broadcasted_iota(jnp.int32, (side, PS), 1) - lax.broadcasted_iota(
        jnp.int32, (side, PS), 0
    )
    inner_r = lax.broadcasted_iota(jnp.int32, (PS, side), 0) - lax.broadcasted_iota(
        jnp.int32, (PS, side), 1
    )
    canvas = jnp.zeros((PS, PS), jnp.float32)
    for t, row_off, col_off in picked:
        col_pick = jnp.where(inner_c == col_off, 1.0, 0.0).astype(jnp.bfloat16)
        row_pick = jnp.where(inner_r == row_off, 1.0, 0.0).astype(jnp.bfloat16)
        moved = jnp.dot(weighted[t], col_pick, preferred_element_type=jnp.float32)
        canvas += jnp.dot(
            row_pick, moved.astype(jnp.bfloat16), preferred_element_type=jnp.float32
        )
    out_ref[0] = canvas.astype(jnp.bfloat16)


def local_canvases(patches, tile_patch, tile_offset, coef_tile, weight_tile, tiles, vtaps, htaps):
    count, side, _ = tiles.shape
    terms, width = vtaps.shape
    half = (width - 1) // 2
    pad = ((0, 0), (0, side - width))
    vline = jnp.roll(jnp.pad(vtaps.astype(jnp.float32), pad), -(half % 8), axis=1)
    hline = jnp.roll(jnp.pad(htaps.astype(jnp.float32)[:, ::-1], pad), -(half % 8), axis=1)
    return pl.pallas_call(
        functools.partial(canvas_kernel, half),
        grid=(patches,),
        out_shape=jax.ShapeDtypeStruct((patches, PS, PS), jnp.bfloat16),
        in_specs=[SMEM] * 5 + [VMEM] * 3,
        out_specs=pl.BlockSpec((1, PS, PS), lambda p: (p, 0, 0)),
        scratch_shapes=[
            pltpu.VMEM((terms, side, side), jnp.bfloat16),
            pltpu.VMEM((terms, side, side), jnp.bfloat16),
            pltpu.VMEM((count, side, side), jnp.bfloat16),
        ],
        compiler_params=pltpu.CompilerParams(vmem_limit_bytes=40 << 20),
    )(
        tile_patch.reshape(-1),
        tile_offset[:, :, 0].reshape(-1),
        tile_offset[:, :, 1].reshape(-1),
        coef_tile.reshape(-1),
        weight_tile,
        tiles,
        vline,
        hline,
    )


def reduce_kernel(
    steps, canvas, out_ref, got1, sum1, got2, sum2, got3, sum3, got4, sends, recvs
):
    e = lax.axis_index("exp")
    g = lax.axis_index("grp")
    hi, lo = e // 2, lax.rem(e, 2)
    far, near = g // 2, lax.rem(g, 2)
    by_core = (e, 2 * far + 1 - near)
    by_x = (e, 2 * (1 - far) + near)
    by_y = (2 * hi + 1 - lo, g)
    goal = [lax.rem(hi + 1 + k, steps) for k in range(steps)]
    by_z = [(2 * goal[k] + lo, g) for k in range(steps - 1)]

    barrier = pltpu.get_barrier_semaphore()
    for partner in [by_core, by_x, by_y] + by_z:
        pl.semaphore_signal(barrier, inc=1, device_id=partner, device_id_type=MESH)
    pl.semaphore_wait(barrier, steps + 2)

    def send(stage, k, src, dst, partner):
        copy = pltpu.make_async_remote_copy(
            src_ref=src,
            dst_ref=dst,
            send_sem=sends.at[stage, k],
            recv_sem=recvs.at[stage, k],
            device_id=partner,
            device_id_type=MESH,
        )
        copy.start()
        return copy

    first = [
        send(0, k, canvas.at[pl.ds(2 * goal[k], 2), :, 1 - near], got1.at[k], by_core)
        for k in range(steps)
    ]
    second, third, fourth = [], [], []
    for k in range(steps):
        first[k].wait_recv()
        sum1[k] = canvas[pl.ds(2 * goal[k], 2), :, near] + got1[k]
        if k % 2 == 0:
            second.append(send(1, k, sum1.at[k, :, 1 - far], got2.at[k], by_x))
        else:
            second.append(send(1, k, sum1.at[k, 1 - lo], got2.at[k], by_y))
    for k in range(steps):
        second[k].wait_recv()
        if k % 2 == 0:
            sum2[k] = sum1[k, :, far] + got2[k]
            third.append(send(2, k, sum2.at[k, 1 - lo], got3.at[k], by_y))
        else:
            sum2[k] = sum1[k, lo] + got2[k]
            third.append(send(2, k, sum2.at[k, 1 - far], got3.at[k], by_x))
    for k in range(steps):
        third[k].wait_recv()
        own = sum2[k, lo] if k % 2 == 0 else sum2[k, far]
        if k < steps - 1:
            sum3[k] = own + got3[k]
            fourth.append(send(3, k, sum3.at[k], got4.at[k], by_z[k]))
        else:
            total = own.astype(jnp.float32) + got3[k].astype(jnp.float32)
    for k in range(steps - 1):
        fourth[k].wait_recv()
        total += got4[k].astype(jnp.float32)
    out_ref[...] = total
    for copy in first + second + third + fourth:
        copy.wait_send()


def reduce_canvases(canvases, n_exp, n_grp):
    rows = PS // n_grp
    if n_grp != 4 or n_exp % 2 or n_exp > 8:
        part = lax.psum_scatter(canvases, "exp", scatter_dimension=0, tiled=True)
        part = lax.psum_scatter(part, "grp", scatter_dimension=1, tiled=True)
        return part[0].astype(jnp.float32)
    steps = n_exp // 2
    kind = canvases.dtype
    return pl.pallas_call(
        functools.partial(reduce_kernel, steps),
        out_shape=jax.ShapeDtypeStruct((rows, PS), jnp.float32),
        in_specs=[VMEM],
        out_specs=VMEM,
        scratch_shapes=[
            pltpu.VMEM((steps, 2, 2, rows, PS), kind),
            pltpu.VMEM((steps, 2, 2, rows, PS), kind),
            pltpu.VMEM((steps, 2, rows, PS), kind),
            pltpu.VMEM((steps, 2, rows, PS), kind),
            pltpu.VMEM((steps, rows, PS), kind),
            pltpu.VMEM((steps - 1, rows, PS), kind),
            pltpu.VMEM((steps - 1, rows, PS), kind),
            pltpu.SemaphoreType.DMA((4, steps)),
            pltpu.SemaphoreType.DMA((4, steps)),
        ],
        compiler_params=pltpu.CompilerParams(
            collective_id=1, has_side_effects=True, vmem_limit_bytes=40 << 20
        ),
    )(canvases.reshape(n_exp, 2, 2, rows, PS))


def fused_kernel(
    shape, exposure_ref, patch_ref, offset_ref, top_ref, tiles_ref, taps_ref, out_ref,
    block, held, vband, hband, weighted, canvas, got1, sum1, got2, sum2, got3, sum3, got4,
    send_a, recv_a, send_b, recv_b, sends, recvs,
):
    n_exp, n_grp, own_rows, half = shape
    steps = n_exp // 2
    terms = vband.shape[0]
    count, side, _ = tiles_ref.shape
    listed = patch_ref.shape[1]
    rows = PS // n_grp
    lines = block.shape[0]
    f32, i32, bf16 = jnp.float32, jnp.int32, jnp.bfloat16
    e = lax.axis_index("exp")
    g = lax.axis_index("grp")
    hi, lo = e // 2, lax.rem(e, 2)
    far, near = g // 2, lax.rem(g, 2)
    by_core = (e, 2 * far + 1 - near)
    by_x = (e, 2 * (1 - far) + near)
    by_y = (2 * hi + 1 - lo, g)
    hops = (2, 1, 3, 0) if steps == 4 else (1, 0)
    goal = [lax.rem(hi + hop, steps) for hop in hops]
    by_z = [(2 * goal[k] + lo, g) for k in range(steps - 1)]
    by_grp = [(e, lax.rem(g + i, n_grp)) for i in range(1, n_grp)]
    by_exp = [(lax.rem(e + i, n_exp), g) for i in range(1, n_exp)]

    barrier = pltpu.get_barrier_semaphore()
    for partner in by_grp + by_exp:
        pl.semaphore_signal(barrier, inc=1, device_id=partner, device_id_type=MESH)

    line = lax.broadcasted_iota(i32, (lines, 128), 0)
    lane = lax.broadcasted_iota(i32, (lines, 128), 1)
    data = top_ref[...]
    for t in range(count):
        values = [exposure_ref[t]] + [patch_ref[t, j] for j in range(listed)]
        values += [offset_ref[t, 2 * j + c] for c in range(2) for j in range(listed)]
        for n, value in enumerate(values):
            data = jnp.where((line == own_rows + t) & (lane == n), value.astype(f32), data)
    block[...] = data
    held[e, g] = data

    pl.semaphore_wait(barrier, n_grp + n_exp - 2)

    def copy_to(src, dst, send_sem, recv_sem, partner):
        copy = pltpu.make_async_remote_copy(
            src_ref=src, dst_ref=dst, send_sem=send_sem, recv_sem=recv_sem,
            device_id=partner, device_id_type=MESH,
        )
        copy.start()
        return copy

    row = lax.broadcasted_iota(i32, (side, side), 0)
    col = lax.broadcasted_iota(i32, (side, side), 1)
    inside = jnp.abs(col - row) <= half

    def build(band, base):
        def one(b, carry):
            taps = jnp.broadcast_to(taps_ref[pl.ds(base + b, 1), :], (side, side))
            taps = pltpu.roll(taps, side - half // 8 * 8, 1, stride=1, stride_axis=0)
            band[b] = jnp.where(inside, taps, 0.0).astype(bf16)
            return carry

        lax.fori_loop(0, terms, one, 0)

    copies = [
        copy_to(block, held.at[e, g], send_a.at[i], recv_a.at[i], partner)
        for i, partner in enumerate(by_grp)
    ]
    build(hband, terms)
    for copy in copies:
        copy.wait()
    copies = [
        copy_to(held.at[e], held.at[e], send_b.at[i], recv_b.at[i], partner)
        for i, partner in enumerate(by_exp)
    ]
    build(vband, 0)
    for copy in copies:
        copy.wait()

    every = held[...].reshape(n_exp * n_grp * lines, 128)
    total_lines = n_exp * n_grp * lines
    spot = lax.broadcasted_iota(i32, (total_lines, 128), 0)
    number = jnp.where(spot % lines < own_rows, spot // lines * own_rows + spot % lines, -1)

    def convolve(t, carry):
        mine = jnp.sum(jnp.where(number == exposure_ref[t], every, 0.0), axis=0, keepdims=True)
        tile = tiles_ref[t]
        total = jnp.zeros((side, side), f32)
        for b in range(terms):
            across = jnp.dot(tile, hband[b], preferred_element_type=f32)
            part = (across * mine[:, b : b + 1]).astype(bf16)
            total += jnp.dot(vband[b], part, preferred_element_type=f32)
        weighted[t] = (mine[:, terms : terms + 1] * total).astype(bf16)
        return carry

    lax.fori_loop(0, count, convolve, 0)

    inner_c = lax.broadcasted_iota(i32, (side, PS), 1) - lax.broadcasted_iota(i32, (side, PS), 0)
    inner_r = lax.broadcasted_iota(i32, (PS, side), 0) - lax.broadcasted_iota(i32, (PS, side), 1)

    def place(k):
        def one(y, carry):
            patch = 2 * goal[k] + y
            picked = [[i32(0), i32(-4 * PS), i32(-4 * PS)] for _ in range(2)]
            found = i32(0)
            for t in range(count):
                for j in range(listed):
                    hit = patch_ref[t, j] == patch
                    new = (i32(t), offset_ref[t, 2 * j], offset_ref[t, 2 * j + 1])
                    for slot in range(2):
                        take = hit & (found == slot)
                        picked[slot] = [
                            jnp.where(take, a, b) for a, b in zip(new, picked[slot])
                        ]
                    found = found + jnp.where(hit, 1, 0)
            image = jnp.zeros((PS, PS), f32)
            for t, row_off, col_off in picked:
                col_pick = jnp.where(inner_c == col_off, 1.0, 0.0).astype(bf16)
                row_pick = jnp.where(inner_r == row_off, 1.0, 0.0).astype(bf16)
                moved = jnp.dot(weighted[t], col_pick, preferred_element_type=f32)
                image += jnp.dot(row_pick, moved.astype(bf16), preferred_element_type=f32)
            canvas[k, y] = image.astype(bf16).reshape(2, 2, rows, PS)
            return carry

        lax.fori_loop(0, 2, one, 0)

    def send(stage, k, src, dst, partner):
        return copy_to(src, dst, sends.at[stage, k], recvs.at[stage, k], partner)

    first, second, rest, third, fourth = [], [], [], [], []

    def first_step(k):
        place(k)
        first.append(send(0, k, canvas.at[k, :, :, 1 - near], got1.at[k], by_core))

    def second_step(k):
        first[k].wait_recv()
        sum1[k] = canvas[k, :, :, near] + got1[k]
        give = sum1.at[k, 1 - lo, 1 - far]
        if k % 2 == 0:
            second.append(send(1, k, give, got2.at[k, 1 - lo], by_x))
            rest.append(send(4, k, sum1.at[k, lo, 1 - far], got2.at[k, lo], by_x))
        else:
            second.append(send(1, k, give, got2.at[k, 1 - far], by_y))
            rest.append(send(4, k, sum1.at[k, 1 - lo, far], got2.at[k, far], by_y))

    def third_step(k):
        second[k].wait_recv()
        if k % 2 == 0:
            sum2[k] = sum1[k, 1 - lo, far] + got2[k, 1 - lo]
        else:
            sum2[k] = sum1[k, lo, 1 - far] + got2[k, 1 - far]
        third.append(send(2, k, sum2.at[k], got3.at[k], by_y if k % 2 == 0 else by_x))

    def owned(k):
        rest[k].wait_recv()
        third[k].wait_recv()
        across = got2[k, lo] if k % 2 == 0 else got2[k, far]
        return sum1[k, lo, far].astype(f32) + across.astype(f32) + got3[k].astype(f32)

    def fourth_step(k):
        sum3[k] = owned(k).astype(bf16)
        fourth.append(send(3, k, sum3.at[k], got4.at[k], by_z[k]))

    first_step(0)
    first_step(1)
    second_step(0)
    second_step(1)
    if steps > 2:
        first_step(2)
    third_step(0)
    third_step(1)
    if steps > 2:
        first_step(3)
        second_step(2)
        second_step(3)

    tag = lambda n: every[:, n : n + 1]
    row_off = jnp.full((total_lines, 1), -4.0 * PS, f32)
    col_off = row_off
    for j in range(listed):
        hit = tag(1 + j) == e.astype(f32)
        row_off = jnp.where(hit, tag(1 + listed + j), row_off)
        col_off = jnp.where(hit, tag(1 + 2 * listed + j), col_off)
    down = lax.broadcasted_iota(i32, (total_lines, total_lines), 1)
    down = jnp.where(down % lines < own_rows, down // lines * own_rows + down % lines, -1)
    chosen = jnp.where(tag(0) == down.astype(f32), 1.0, 0.0).astype(bf16)
    weights = jnp.dot(chosen, every.astype(bf16), preferred_element_type=f32)
    weights = weights[:, terms : terms + 1]
    kept = lax.broadcasted_iota(i32, (total_lines, 1), 0) % lines
    weights = jnp.where((kept >= own_rows) & (kept < own_rows + count), weights, 0.0)
    y = (lax.broadcasted_iota(i32, (total_lines, rows), 1) + g * rows).astype(f32)
    x = lax.broadcasted_iota(i32, (total_lines, PS), 1).astype(f32)
    row_mask = jnp.where((y >= row_off) & (y < row_off + side), weights, 0.0).astype(bf16)
    col_mask = jnp.where((x >= col_off) & (x < col_off + side), 1.0, 0.0).astype(bf16)
    cover = lax.dot_general(
        row_mask, col_mask, (((0,), (0,)), ((), ())), preferred_element_type=f32
    )
    out_ref[0] = jnp.maximum(cover, 1.0)

    fourth_step(0)
    if steps > 2:
        fourth_step(1)
        third_step(2)
        third_step(3)
        fourth_step(2)
    total = owned(steps - 1)
    for k in range(steps - 1):
        fourth[k].wait_recv()
        total += got4[k].astype(f32)
    out_ref[0] = total / out_ref[0]
    for copy in first + second + rest + third + fourth:
        copy.wait_send()


def fused(
    n_exp, n_grp, tiles, tile_exposure, tile_patch, tile_offset, coeffs, inv_var, vtaps, htaps
):
    count, side, _ = tiles.shape
    terms, width = vtaps.shape
    half = (width - 1) // 2
    own_rows = coeffs.shape[0]
    lines = -(-(own_rows + count) // 8) * 8
    rows = PS // n_grp
    steps = n_exp // 2
    f32, kind = jnp.float32, jnp.bfloat16
    top = jnp.concatenate([coeffs, inv_var[:, None]], axis=1).astype(f32)
    top = jnp.pad(top, ((0, lines - own_rows), (0, 128 - terms - 1)))
    taps = jnp.concatenate([vtaps, htaps[:, ::-1]], axis=0).astype(f32)
    taps = jnp.concatenate(
        [
            taps[:, half % 8 :],
            jnp.zeros((2 * terms, side - width), f32),
            taps[:, : half % 8],
        ],
        axis=1,
    )
    dma = pltpu.SemaphoreType.DMA
    return pl.pallas_call(
        functools.partial(fused_kernel, (n_exp, n_grp, own_rows, half)),
        out_shape=jax.ShapeDtypeStruct((1, rows, PS), f32),
        in_specs=[SMEM] * 3 + [VMEM] * 3,
        out_specs=VMEM,
        scratch_shapes=[
            pltpu.VMEM((lines, 128), f32),
            pltpu.VMEM((n_exp, n_grp, lines, 128), f32),
            pltpu.VMEM((terms, side, side), kind),
            pltpu.VMEM((terms, side, side), kind),
            pltpu.VMEM((count, side, side), kind),
            pltpu.VMEM((steps, 2, 2, 2, rows, PS), kind),
            pltpu.VMEM((steps, 2, 2, rows, PS), kind),
            pltpu.VMEM((steps, 2, 2, rows, PS), kind),
            pltpu.VMEM((steps, 2, rows, PS), kind),
            pltpu.VMEM((steps, rows, PS), kind),
            pltpu.VMEM((steps, rows, PS), kind),
            pltpu.VMEM((steps - 1, rows, PS), kind),
            pltpu.VMEM((steps - 1, rows, PS), kind),
            dma((n_grp - 1,)),
            dma((n_grp - 1,)),
            dma((n_exp - 1,)),
            dma((n_exp - 1,)),
            dma((5, steps)),
            dma((5, steps)),
        ],
        compiler_params=pltpu.CompilerParams(
            collective_id=2, has_side_effects=True, vmem_limit_bytes=48 << 20
        ),
    )(tile_exposure, tile_patch, tile_offset.reshape(count, -1), top, tiles, taps)


def per_device(
    tiles, tile_exposure, tile_patch, tile_offset, coeffs, inv_var, vert_taps, horiz_taps
):
    n_exp = lax.axis_size("exp")
    n_grp = lax.axis_size("grp")
    count, side, _ = tiles.shape
    listed = tile_patch.shape[1]
    held, terms = coeffs.shape
    f32 = jnp.float32
    if n_grp == 4 and n_exp in (4, 8):
        return fused(
            n_exp, n_grp, tiles, tile_exposure, tile_patch, tile_offset, coeffs, inv_var,
            vert_taps, horiz_taps,
        )
    top = jnp.concatenate([coeffs, inv_var[:, None]], axis=1).astype(f32)
    low = jnp.concatenate(
        [tile_exposure[:, None], tile_patch, tile_offset[:, :, 0], tile_offset[:, :, 1]], axis=1
    ).astype(f32)
    lines = -(-(held + count) // 8) * 8
    block = jnp.concatenate(
        [
            jnp.pad(top, ((0, 0), (0, 128 - top.shape[1]))),
            jnp.pad(low, ((0, lines - held - count), (0, 128 - low.shape[1]))),
        ],
        axis=0,
    )
    every = gather_blocks(block, n_exp, n_grp).reshape(n_exp * n_grp, lines, 128)
    table = every[:, :held, : terms + 1].reshape(-1, terms + 1).astype(jnp.bfloat16)
    tags = every[:, held : held + count, : low.shape[1]].reshape(-1, low.shape[1])
    names = tags[:, 0].astype(jnp.int32)
    exposures = jnp.arange(table.shape[0], dtype=jnp.int32)
    mine = jnp.dot(
        (tile_exposure[:, None] == exposures[None, :]).astype(jnp.bfloat16),
        table,
        preferred_element_type=f32,
    )
    canvases = local_canvases(
        n_exp, tile_patch, tile_offset, mine[:, :terms], mine[:, terms], tiles, vert_taps, horiz_taps
    )

    weights = jnp.dot(
        (names[:, None] == exposures[None, :]).astype(jnp.bfloat16),
        table[:, terms:],
        preferred_element_type=f32,
    )
    here = (tags[:, 1 : 1 + listed] == lax.axis_index("exp").astype(f32)).astype(f32)
    named = jnp.sum(here, axis=1, keepdims=True) > 0
    row_off = jnp.sum(here * tags[:, 1 + listed : 1 + 2 * listed], axis=1, keepdims=True)
    col_off = jnp.sum(here * tags[:, 1 + 2 * listed : 1 + 3 * listed], axis=1, keepdims=True)
    rows = PS // n_grp
    y = (jnp.arange(rows, dtype=jnp.int32) + lax.axis_index("grp") * rows).astype(f32)[None, :]
    x = jnp.arange(PS, dtype=jnp.int32).astype(f32)[None, :]
    row_mask = jnp.where(named & (y >= row_off) & (y < row_off + side), weights, 0.0)
    col_mask = (x >= col_off) & (x < col_off + side)
    cover = lax.dot_general(
        row_mask.astype(jnp.bfloat16),
        col_mask.astype(jnp.bfloat16),
        (((0,), (0,)), ((), ())),
        preferred_element_type=f32,
    )
    flux = reduce_canvases(canvases, n_exp, n_grp)
    return (flux / jnp.maximum(cover, 1.0))[None]


def solution(mesh):
    in_specs = (
        P(("exp", "grp"), None, None),
        P(("exp", "grp")),
        P(("exp", "grp"), None),
        P(("exp", "grp"), None, None),
        P(("exp", "grp"), None),
        P(("exp", "grp")),
        P(),
        P(),
    )
    out_specs = P("exp", "grp", None)
    return jax.shard_map(
        per_device, mesh=mesh, in_specs=in_specs, out_specs=out_specs, check_vma=False
    )
```

```python
import functools

import jax
import jax.numpy as jnp
from jax import lax
from jax.experimental import pallas as pl
from jax.experimental.pallas import tpu as pltpu
from jax.sharding import PartitionSpec as P

PS = 512
MESH = pl.DeviceIdType.MESH
VMEM = pl.BlockSpec(memory_space=pltpu.VMEM)
SMEM = pl.BlockSpec(memory_space=pltpu.SMEM)


def gather_kernel(n_exp, n_grp, block_ref, out_ref, held, send_a, recv_a, send_b, recv_b):
    e = lax.axis_index("exp")
    g = lax.axis_index("grp")
    barrier = pltpu.get_barrier_semaphore()
    for i in range(1, n_grp):
        pl.semaphore_signal(
            barrier, inc=1, device_id=(e, lax.rem(g + i, n_grp)), device_id_type=MESH
        )
    for i in range(1, n_exp):
        pl.semaphore_signal(
            barrier, inc=1, device_id=(lax.rem(e + i, n_exp), g), device_id_type=MESH
        )
    pl.semaphore_wait(barrier, n_grp + n_exp - 2)

    held[e, g] = block_ref[...]
    copies = []
    for i in range(1, n_grp):
        copy = pltpu.make_async_remote_copy(
            src_ref=block_ref,
            dst_ref=held.at[e, g],
            send_sem=send_a.at[i - 1],
            recv_sem=recv_a.at[i - 1],
            device_id=(e, lax.rem(g + i, n_grp)),
            device_id_type=MESH,
        )
        copy.start()
        copies.append(copy)
    for copy in copies:
        copy.wait()
    copies = []
    for i in range(1, n_exp):
        copy = pltpu.make_async_remote_copy(
            src_ref=held.at[e],
            dst_ref=held.at[e],
            send_sem=send_b.at[i - 1],
            recv_sem=recv_b.at[i - 1],
            device_id=(lax.rem(e + i, n_exp), g),
            device_id_type=MESH,
        )
        copy.start()
        copies.append(copy)
    for copy in copies:
        copy.wait()
    out_ref[...] = held[...]


def gather_blocks(block, n_exp, n_grp):
    shape = (n_exp, n_grp) + block.shape
    return pl.pallas_call(
        functools.partial(gather_kernel, n_exp, n_grp),
        out_shape=jax.ShapeDtypeStruct(shape, block.dtype),
        in_specs=[VMEM],
        out_specs=VMEM,
        scratch_shapes=[
            pltpu.VMEM(shape, block.dtype),
            pltpu.SemaphoreType.DMA((n_grp - 1,)),
            pltpu.SemaphoreType.DMA((n_grp - 1,)),
            pltpu.SemaphoreType.DMA((n_exp - 1,)),
            pltpu.SemaphoreType.DMA((n_exp - 1,)),
        ],
        compiler_params=pltpu.CompilerParams(collective_id=0, has_side_effects=True),
    )(block)


def canvas_kernel(
    half, patch_ref, row_ref, col_ref, coef_ref, weight_ref, tiles_ref, vtap_ref, htap_ref,
    out_ref, vband, hband, weighted,
):
    terms, side = vtap_ref.shape
    count = tiles_ref.shape[0]
    listed = patch_ref.shape[0] // count
    patch = pl.program_id(0)

    @pl.when(patch == 0)
    def _():
        row = lax.broadcasted_iota(jnp.int32, (side, side), 0)
        col = lax.broadcasted_iota(jnp.int32, (side, side), 1)
        inside = jnp.abs(col - row) <= half

        def build(b, carry):
            for taps, band in ((vtap_ref, vband), (htap_ref, hband)):
                line = jnp.broadcast_to(taps[pl.ds(b, 1), :], (side, side))
                line = pltpu.roll(line, side - half // 8 * 8, 1, stride=1, stride_axis=0)
                band[b] = jnp.where(inside, line, 0.0).astype(jnp.bfloat16)
            return carry

        lax.fori_loop(0, terms, build, 0)

        def convolve(t, carry):
            tile = tiles_ref[t]
            total = jnp.zeros((side, side), jnp.float32)
            for b in range(terms):
                across = jnp.dot(tile, hband[b], preferred_element_type=jnp.float32)
                part = (across * coef_ref[t * terms + b]).astype(jnp.bfloat16)
                total += jnp.dot(vband[b], part, preferred_element_type=jnp.float32)
            weighted[t] = (weight_ref[t] * total).astype(jnp.bfloat16)
            return carry

        lax.fori_loop(0, count, convolve, 0)

    far = -4 * PS
    picked = [[jnp.int32(0), jnp.int32(far), jnp.int32(far)] for _ in range(2)]
    found = jnp.int32(0)
    for t in range(count):
        for j in range(listed):
            n = t * listed + j
            hit = patch_ref[n] == patch
            for slot in range(2):
                take = hit & (found == slot)
                picked[slot] = [
                    jnp.where(take, new, old)
                    for new, old in zip((t, row_ref[n], col_ref[n]), picked[slot])
                ]
            found = found + hit.astype(jnp.int32)

    inner_c = lax.broadcasted_iota(jnp.int32, (side, PS), 1) - lax.broadcasted_iota(
        jnp.int32, (side, PS), 0
    )
    inner_r = lax.broadcasted_iota(jnp.int32, (PS, side), 0) - lax.broadcasted_iota(
        jnp.int32, (PS, side), 1
    )
    canvas = jnp.zeros((PS, PS), jnp.float32)
    for t, row_off, col_off in picked:
        col_pick = jnp.where(inner_c == col_off, 1.0, 0.0).astype(jnp.bfloat16)
        row_pick = jnp.where(inner_r == row_off, 1.0, 0.0).astype(jnp.bfloat16)
        moved = jnp.dot(weighted[t], col_pick, preferred_element_type=jnp.float32)
        canvas += jnp.dot(
            row_pick, moved.astype(jnp.bfloat16), preferred_element_type=jnp.float32
        )
    out_ref[0] = canvas.astype(jnp.bfloat16)


def local_canvases(patches, tile_patch, tile_offset, coef_tile, weight_tile, tiles, vtaps, htaps):
    count, side, _ = tiles.shape
    terms, width = vtaps.shape
    half = (width - 1) // 2
    pad = ((0, 0), (0, side - width))
    vline = jnp.roll(jnp.pad(vtaps.astype(jnp.float32), pad), -(half % 8), axis=1)
    hline = jnp.roll(jnp.pad(htaps.astype(jnp.float32)[:, ::-1], pad), -(half % 8), axis=1)
    return pl.pallas_call(
        functools.partial(canvas_kernel, half),
        grid=(patches,),
        out_shape=jax.ShapeDtypeStruct((patches, PS, PS), jnp.bfloat16),
        in_specs=[SMEM] * 5 + [VMEM] * 3,
        out_specs=pl.BlockSpec((1, PS, PS), lambda p: (p, 0, 0)),
        scratch_shapes=[
            pltpu.VMEM((terms, side, side), jnp.bfloat16),
            pltpu.VMEM((terms, side, side), jnp.bfloat16),
            pltpu.VMEM((count, side, side), jnp.bfloat16),
        ],
        compiler_params=pltpu.CompilerParams(vmem_limit_bytes=40 << 20),
    )(
        tile_patch.reshape(-1),
        tile_offset[:, :, 0].reshape(-1),
        tile_offset[:, :, 1].reshape(-1),
        coef_tile.reshape(-1),
        weight_tile,
        tiles,
        vline,
        hline,
    )


def reduce_kernel(
    steps, canvas, out_ref, got1, sum1, got2, sum2, got3, sum3, got4, sends, recvs
):
    e = lax.axis_index("exp")
    g = lax.axis_index("grp")
    hi, lo = e // 2, lax.rem(e, 2)
    far, near = g // 2, lax.rem(g, 2)
    by_core = (e, 2 * far + 1 - near)
    by_x = (e, 2 * (1 - far) + near)
    by_y = (2 * hi + 1 - lo, g)
    goal = [lax.rem(hi + 1 + k, steps) for k in range(steps)]
    by_z = [(2 * goal[k] + lo, g) for k in range(steps - 1)]

    barrier = pltpu.get_barrier_semaphore()
    for partner in [by_core, by_x, by_y] + by_z:
        pl.semaphore_signal(barrier, inc=1, device_id=partner, device_id_type=MESH)
    pl.semaphore_wait(barrier, steps + 2)

    def send(stage, k, src, dst, partner):
        copy = pltpu.make_async_remote_copy(
            src_ref=src,
            dst_ref=dst,
            send_sem=sends.at[stage, k],
            recv_sem=recvs.at[stage, k],
            device_id=partner,
            device_id_type=MESH,
        )
        copy.start()
        return copy

    first = [
        send(0, k, canvas.at[pl.ds(2 * goal[k], 2), :, 1 - near], got1.at[k], by_core)
        for k in range(steps)
    ]
    second, third, fourth = [], [], []
    for k in range(steps):
        first[k].wait_recv()
        sum1[k] = canvas[pl.ds(2 * goal[k], 2), :, near] + got1[k]
        if k % 2 == 0:
            second.append(send(1, k, sum1.at[k, :, 1 - far], got2.at[k], by_x))
        else:
            second.append(send(1, k, sum1.at[k, 1 - lo], got2.at[k], by_y))
    for k in range(steps):
        second[k].wait_recv()
        if k % 2 == 0:
            sum2[k] = sum1[k, :, far] + got2[k]
            third.append(send(2, k, sum2.at[k, 1 - lo], got3.at[k], by_y))
        else:
            sum2[k] = sum1[k, lo] + got2[k]
            third.append(send(2, k, sum2.at[k, 1 - far], got3.at[k], by_x))
    for k in range(steps):
        third[k].wait_recv()
        own = sum2[k, lo] if k % 2 == 0 else sum2[k, far]
        if k < steps - 1:
            sum3[k] = own + got3[k]
            fourth.append(send(3, k, sum3.at[k], got4.at[k], by_z[k]))
        else:
            total = own.astype(jnp.float32) + got3[k].astype(jnp.float32)
    for k in range(steps - 1):
        fourth[k].wait_recv()
        total += got4[k].astype(jnp.float32)
    out_ref[...] = total
    for copy in first + second + third + fourth:
        copy.wait_send()


def reduce_canvases(canvases, n_exp, n_grp):
    rows = PS // n_grp
    if n_grp != 4 or n_exp % 2 or n_exp > 8:
        part = lax.psum_scatter(canvases, "exp", scatter_dimension=0, tiled=True)
        part = lax.psum_scatter(part, "grp", scatter_dimension=1, tiled=True)
        return part[0].astype(jnp.float32)
    steps = n_exp // 2
    kind = canvases.dtype
    return pl.pallas_call(
        functools.partial(reduce_kernel, steps),
        out_shape=jax.ShapeDtypeStruct((rows, PS), jnp.float32),
        in_specs=[VMEM],
        out_specs=VMEM,
        scratch_shapes=[
            pltpu.VMEM((steps, 2, 2, rows, PS), kind),
            pltpu.VMEM((steps, 2, 2, rows, PS), kind),
            pltpu.VMEM((steps, 2, rows, PS), kind),
            pltpu.VMEM((steps, 2, rows, PS), kind),
            pltpu.VMEM((steps, rows, PS), kind),
            pltpu.VMEM((steps - 1, rows, PS), kind),
            pltpu.VMEM((steps - 1, rows, PS), kind),
            pltpu.SemaphoreType.DMA((4, steps)),
            pltpu.SemaphoreType.DMA((4, steps)),
        ],
        compiler_params=pltpu.CompilerParams(
            collective_id=1, has_side_effects=True, vmem_limit_bytes=40 << 20
        ),
    )(canvases.reshape(n_exp, 2, 2, rows, PS))


def fused_kernel(
    shape, exposure_ref, patch_ref, offset_ref, top_ref, tiles_hbm, taps_ref, out_ref,
    block, held, vband, hband, weighted, canvas, got1, sum1, got2, sum2, got3, sum3, got4,
    send_a, recv_a, send_b, recv_b, sends, recvs, tiles_ref, tiles_sem,
):
    n_exp, n_grp, own_rows, half = shape
    steps = n_exp // 2
    terms = vband.shape[0]
    count, side, _ = tiles_ref.shape
    listed = patch_ref.shape[1]
    rows = PS // n_grp
    lines = block.shape[0]
    f32, i32, bf16 = jnp.float32, jnp.int32, jnp.bfloat16
    e = lax.axis_index("exp")
    g = lax.axis_index("grp")
    hi, lo = e // 2, lax.rem(e, 2)
    far, near = g // 2, lax.rem(g, 2)
    by_core = (e, 2 * far + 1 - near)
    by_x = (e, 2 * (1 - far) + near)
    by_y = (2 * hi + 1 - lo, g)
    hops = (2, 1, 3, 0) if steps == 4 else (1, 0)
    goal = [lax.rem(hi + hop, steps) for hop in hops]
    by_z = [(2 * goal[k] + lo, g) for k in range(steps - 1)]
    by_grp = [(e, lax.rem(g + i, n_grp)) for i in range(1, n_grp)]
    by_exp = [(lax.rem(e + i, n_exp), g) for i in range(1, n_exp)]

    fetch = pltpu.make_async_copy(tiles_hbm, tiles_ref, tiles_sem)
    fetch.start()
    barrier = pltpu.get_barrier_semaphore()
    for partner in by_grp + by_exp:
        pl.semaphore_signal(barrier, inc=1, device_id=partner, device_id_type=MESH)

    line = lax.broadcasted_iota(i32, (lines, 128), 0)
    lane = lax.broadcasted_iota(i32, (lines, 128), 1)
    data = top_ref[...]
    for t in range(count):
        values = [exposure_ref[t]] + [patch_ref[t, j] for j in range(listed)]
        values += [offset_ref[t, 2 * j + c] for c in range(2) for j in range(listed)]
        for n, value in enumerate(values):
            data = jnp.where((line == own_rows + t) & (lane == n), value.astype(f32), data)
    block[...] = data
    held[e, g] = data

    pl.semaphore_wait(barrier, n_grp + n_exp - 2)

    def copy_to(src, dst, send_sem, recv_sem, partner):
        copy = pltpu.make_async_remote_copy(
            src_ref=src, dst_ref=dst, send_sem=send_sem, recv_sem=recv_sem,
            device_id=partner, device_id_type=MESH,
        )
        copy.start()
        return copy

    row = lax.broadcasted_iota(i32, (side, side), 0)
    col = lax.broadcasted_iota(i32, (side, side), 1)
    inside = jnp.abs(col - row) <= half

    def build(band, base):
        def one(b, carry):
            taps = jnp.broadcast_to(taps_ref[pl.ds(base + b, 1), :], (side, side))
            taps = pltpu.roll(taps, side - half // 8 * 8, 1, stride=1, stride_axis=0)
            band[b] = jnp.where(inside, taps, 0.0).astype(bf16)
            return carry

        lax.fori_loop(0, terms, one, 0)

    copies = [
        copy_to(block, held.at[e, g], send_a.at[i], recv_a.at[i], partner)
        for i, partner in enumerate(by_grp)
    ]
    build(hband, terms)
    for copy in copies:
        copy.wait()
    copies = [
        copy_to(held.at[e], held.at[e], send_b.at[i], recv_b.at[i], partner)
        for i, partner in enumerate(by_exp)
    ]
    build(vband, 0)
    for copy in copies:
        copy.wait()

    every = held[...].reshape(n_exp * n_grp * lines, 128)
    total_lines = n_exp * n_grp * lines
    spot = lax.broadcasted_iota(i32, (total_lines, 128), 0)
    number = jnp.where(spot % lines < own_rows, spot // lines * own_rows + spot % lines, -1)

    def convolve(t, carry):
        mine = jnp.sum(jnp.where(number == exposure_ref[t], every, 0.0), axis=0, keepdims=True)
        tile = tiles_ref[t]
        total = jnp.zeros((side, side), f32)
        for b in range(terms):
            across = jnp.dot(tile, hband[b], preferred_element_type=f32)
            part = (across * mine[:, b : b + 1]).astype(bf16)
            total += jnp.dot(vband[b], part, preferred_element_type=f32)
        weighted[t] = (mine[:, terms : terms + 1] * total).astype(bf16)
        return carry

    fetch.wait()
    lax.fori_loop(0, count, convolve, 0)

    inner_c = lax.broadcasted_iota(i32, (side, PS), 1) - lax.broadcasted_iota(i32, (side, PS), 0)
    inner_r = lax.broadcasted_iota(i32, (PS, side), 0) - lax.broadcasted_iota(i32, (PS, side), 1)

    def place(k):
        def one(y, carry):
            patch = 2 * goal[k] + y
            picked = [[i32(0), i32(-4 * PS), i32(-4 * PS)] for _ in range(2)]
            found = i32(0)
            for t in range(count):
                for j in range(listed):
                    hit = patch_ref[t, j] == patch
                    new = (i32(t), offset_ref[t, 2 * j], offset_ref[t, 2 * j + 1])
                    for slot in range(2):
                        take = hit & (found == slot)
                        picked[slot] = [
                            jnp.where(take, a, b) for a, b in zip(new, picked[slot])
                        ]
                    found = found + jnp.where(hit, 1, 0)
            image = jnp.zeros((PS, PS), f32)
            for t, row_off, col_off in picked:
                col_pick = jnp.where(inner_c == col_off, 1.0, 0.0).astype(bf16)
                row_pick = jnp.where(inner_r == row_off, 1.0, 0.0).astype(bf16)
                moved = jnp.dot(weighted[t], col_pick, preferred_element_type=f32)
                image += jnp.dot(row_pick, moved.astype(bf16), preferred_element_type=f32)
            canvas[k, y] = image.astype(bf16).reshape(2, 2, rows, PS)
            return carry

        lax.fori_loop(0, 2, one, 0)

    def send(stage, k, src, dst, partner):
        return copy_to(src, dst, sends.at[stage, k], recvs.at[stage, k], partner)

    first, second, rest, third, fourth = [], [], [], [], []

    def first_step(k):
        place(k)
        first.append(send(0, k, canvas.at[k, :, :, 1 - near], got1.at[k], by_core))

    def second_step(k):
        first[k].wait_recv()
        sum1[k] = canvas[k, :, :, near] + got1[k]
        give = sum1.at[k, 1 - lo, 1 - far]
        if k % 2 == 0:
            second.append(send(1, k, give, got2.at[k, 1 - lo], by_x))
            rest.append(send(4, k, sum1.at[k, lo, 1 - far], got2.at[k, lo], by_x))
        else:
            second.append(send(1, k, give, got2.at[k, 1 - far], by_y))
            rest.append(send(4, k, sum1.at[k, 1 - lo, far], got2.at[k, far], by_y))

    def third_step(k):
        second[k].wait_recv()
        if k % 2 == 0:
            sum2[k] = sum1[k, 1 - lo, far] + got2[k, 1 - lo]
        else:
            sum2[k] = sum1[k, lo, 1 - far] + got2[k, 1 - far]
        third.append(send(2, k, sum2.at[k], got3.at[k], by_y if k % 2 == 0 else by_x))

    def owned(k):
        rest[k].wait_recv()
        third[k].wait_recv()
        across = got2[k, lo] if k % 2 == 0 else got2[k, far]
        return sum1[k, lo, far].astype(f32) + across.astype(f32) + got3[k].astype(f32)

    def fourth_step(k):
        sum3[k] = owned(k).astype(bf16)
        fourth.append(send(3, k, sum3.at[k], got4.at[k], by_z[k]))

    first_step(0)
    first_step(1)
    second_step(0)
    second_step(1)
    if steps > 2:
        first_step(2)
    third_step(0)
    third_step(1)
    if steps > 2:
        first_step(3)
        second_step(2)
        second_step(3)

    tag = lambda n: every[:, n : n + 1]
    row_off = jnp.full((total_lines, 1), -4.0 * PS, f32)
    col_off = row_off
    for j in range(listed):
        hit = tag(1 + j) == e.astype(f32)
        row_off = jnp.where(hit, tag(1 + listed + j), row_off)
        col_off = jnp.where(hit, tag(1 + 2 * listed + j), col_off)
    down = lax.broadcasted_iota(i32, (total_lines, total_lines), 1)
    down = jnp.where(down % lines < own_rows, down // lines * own_rows + down % lines, -1)
    chosen = jnp.where(tag(0) == down.astype(f32), 1.0, 0.0).astype(bf16)
    weights = jnp.dot(chosen, every.astype(bf16), preferred_element_type=f32)
    weights = weights[:, terms : terms + 1]
    kept = lax.broadcasted_iota(i32, (total_lines, 1), 0) % lines
    weights = jnp.where((kept >= own_rows) & (kept < own_rows + count), weights, 0.0)
    y = (lax.broadcasted_iota(i32, (total_lines, rows), 1) + g * rows).astype(f32)
    x = lax.broadcasted_iota(i32, (total_lines, PS), 1).astype(f32)
    row_mask = jnp.where((y >= row_off) & (y < row_off + side), weights, 0.0).astype(bf16)
    col_mask = jnp.where((x >= col_off) & (x < col_off + side), 1.0, 0.0).astype(bf16)
    cover = lax.dot_general(
        row_mask, col_mask, (((0,), (0,)), ((), ())), preferred_element_type=f32
    )
    out_ref[0] = jnp.maximum(cover, 1.0)

    fourth_step(0)
    if steps > 2:
        fourth_step(1)
        third_step(2)
        third_step(3)
        fourth_step(2)
    total = owned(steps - 1)
    for k in range(steps - 1):
        fourth[k].wait_recv()
        total += got4[k].astype(f32)
    out_ref[0] = total / out_ref[0]
    for copy in first + second + rest + third + fourth:
        copy.wait_send()


def fused(
    n_exp, n_grp, tiles, tile_exposure, tile_patch, tile_offset, coeffs, inv_var, vtaps, htaps
):
    count, side, _ = tiles.shape
    terms, width = vtaps.shape
    half = (width - 1) // 2
    own_rows = coeffs.shape[0]
    lines = -(-(own_rows + count) // 8) * 8
    rows = PS // n_grp
    steps = n_exp // 2
    f32, kind = jnp.float32, jnp.bfloat16
    top = jnp.concatenate([coeffs, inv_var[:, None]], axis=1).astype(f32)
    top = jnp.pad(top, ((0, lines - own_rows), (0, 128 - terms - 1)))
    taps = jnp.concatenate([vtaps, htaps[:, ::-1]], axis=0).astype(f32)
    taps = jnp.concatenate(
        [
            taps[:, half % 8 :],
            jnp.zeros((2 * terms, side - width), f32),
            taps[:, : half % 8],
        ],
        axis=1,
    )
    dma = pltpu.SemaphoreType.DMA
    return pl.pallas_call(
        functools.partial(fused_kernel, (n_exp, n_grp, own_rows, half)),
        out_shape=jax.ShapeDtypeStruct((1, rows, PS), f32),
        in_specs=[SMEM] * 3 + [VMEM, pl.BlockSpec(memory_space=pltpu.HBM), VMEM],
        out_specs=VMEM,
        scratch_shapes=[
            pltpu.VMEM((lines, 128), f32),
            pltpu.VMEM((n_exp, n_grp, lines, 128), f32),
            pltpu.VMEM((terms, side, side), kind),
            pltpu.VMEM((terms, side, side), kind),
            pltpu.VMEM((count, side, side), kind),
            pltpu.VMEM((steps, 2, 2, 2, rows, PS), kind),
            pltpu.VMEM((steps, 2, 2, rows, PS), kind),
            pltpu.VMEM((steps, 2, 2, rows, PS), kind),
            pltpu.VMEM((steps, 2, rows, PS), kind),
            pltpu.VMEM((steps, rows, PS), kind),
            pltpu.VMEM((steps, rows, PS), kind),
            pltpu.VMEM((steps - 1, rows, PS), kind),
            pltpu.VMEM((steps - 1, rows, PS), kind),
            dma((n_grp - 1,)),
            dma((n_grp - 1,)),
            dma((n_exp - 1,)),
            dma((n_exp - 1,)),
            dma((5, steps)),
            dma((5, steps)),
            pltpu.VMEM(tiles.shape, tiles.dtype),
            dma,
        ],
        compiler_params=pltpu.CompilerParams(
            collective_id=2, has_side_effects=True, vmem_limit_bytes=(64 << 20) - (256 << 10)
        ),
    )(tile_exposure, tile_patch, tile_offset.reshape(count, -1), top, tiles, taps)


def per_device(
    tiles, tile_exposure, tile_patch, tile_offset, coeffs, inv_var, vert_taps, horiz_taps
):
    n_exp = lax.axis_size("exp")
    n_grp = lax.axis_size("grp")
    count, side, _ = tiles.shape
    listed = tile_patch.shape[1]
    held, terms = coeffs.shape
    f32 = jnp.float32
    if n_grp == 4 and n_exp in (4, 8):
        return fused(
            n_exp, n_grp, tiles, tile_exposure, tile_patch, tile_offset, coeffs, inv_var,
            vert_taps, horiz_taps,
        )
    top = jnp.concatenate([coeffs, inv_var[:, None]], axis=1).astype(f32)
    low = jnp.concatenate(
        [tile_exposure[:, None], tile_patch, tile_offset[:, :, 0], tile_offset[:, :, 1]], axis=1
    ).astype(f32)
    lines = -(-(held + count) // 8) * 8
    block = jnp.concatenate(
        [
            jnp.pad(top, ((0, 0), (0, 128 - top.shape[1]))),
            jnp.pad(low, ((0, lines - held - count), (0, 128 - low.shape[1]))),
        ],
        axis=0,
    )
    every = gather_blocks(block, n_exp, n_grp).reshape(n_exp * n_grp, lines, 128)
    table = every[:, :held, : terms + 1].reshape(-1, terms + 1).astype(jnp.bfloat16)
    tags = every[:, held : held + count, : low.shape[1]].reshape(-1, low.shape[1])
    names = tags[:, 0].astype(jnp.int32)
    exposures = jnp.arange(table.shape[0], dtype=jnp.int32)
    mine = jnp.dot(
        (tile_exposure[:, None] == exposures[None, :]).astype(jnp.bfloat16),
        table,
        preferred_element_type=f32,
    )
    canvases = local_canvases(
        n_exp, tile_patch, tile_offset, mine[:, :terms], mine[:, terms], tiles, vert_taps, horiz_taps
    )

    weights = jnp.dot(
        (names[:, None] == exposures[None, :]).astype(jnp.bfloat16),
        table[:, terms:],
        preferred_element_type=f32,
    )
    here = (tags[:, 1 : 1 + listed] == lax.axis_index("exp").astype(f32)).astype(f32)
    named = jnp.sum(here, axis=1, keepdims=True) > 0
    row_off = jnp.sum(here * tags[:, 1 + listed : 1 + 2 * listed], axis=1, keepdims=True)
    col_off = jnp.sum(here * tags[:, 1 + 2 * listed : 1 + 3 * listed], axis=1, keepdims=True)
    rows = PS // n_grp
    y = (jnp.arange(rows, dtype=jnp.int32) + lax.axis_index("grp") * rows).astype(f32)[None, :]
    x = jnp.arange(PS, dtype=jnp.int32).astype(f32)[None, :]
    row_mask = jnp.where(named & (y >= row_off) & (y < row_off + side), weights, 0.0)
    col_mask = (x >= col_off) & (x < col_off + side)
    cover = lax.dot_general(
        row_mask.astype(jnp.bfloat16),
        col_mask.astype(jnp.bfloat16),
        (((0,), (0,)), ((), ())),
        preferred_element_type=f32,
    )
    flux = reduce_canvases(canvases, n_exp, n_grp)
    return (flux / jnp.maximum(cover, 1.0))[None]


def solution(mesh):
    in_specs = (
        P(("exp", "grp"), None, None),
        P(("exp", "grp")),
        P(("exp", "grp"), None),
        P(("exp", "grp"), None, None),
        P(("exp", "grp"), None),
        P(("exp", "grp")),
        P(),
        P(),
    )
    out_specs = P("exp", "grp", None)
    return jax.shard_map(
        per_device, mesh=mesh, in_specs=in_specs, out_specs=out_specs, check_vma=False
    )
```
